512 devices in a mesh: space: 64 (over y, z), mem: 8 (over x, core).
Axes of the slice: x: 4, y: 4, z: 16, core: 2. Of those that a mesh axis runs over, the one named last changes fastest.
Arguments:
- prior_state: bfloat16 [256, 786432], P('mem', 'space'), may hold values from -6 to 6
- block_counts: int32 [2, 64], P(None, 'space'), may hold values from 1 to 4, 128 in all within a row
- block_index: int32 [2, 256], P(None, 'space'), may hold values from 0 to 95
- gate_operator: float32 [2, 256, 32, 128], P(None, 'space'), may hold values from -0.5 to 0.5
- observed: float32 [2, 8192], P(None, 'space'), may hold values from -8 to 8
- obs_error: float32 [2, 8192], P(None, 'space'), may hold values from 0.25 to 4
- local_mask: int32 [2, 6144, 20], P(None, 'space'), may hold values 0 or 1
Outputs:
- analysis: bfloat16 [256, 786432], P('mem', 'space')
The draws below stay inside these ranges and needn't reach their ends.
Inputs may be any that keep to these rules, and one draw needn't show every extreme that they name: `block_counts`: in each batch the counts over all tiles sum to twice the number of tiles, and some tile holds exactly 4.
All inputs are finite; a program needn't handle non-finite values. No bound on the sum of `block_counts` or of `local_mask` on one device may be relied on, other than what follows from the above.
Results may differ from the reference program's by a relative error of at most 0.0055.
Values may be sent and summed in bfloat16 or wider, within the bound.
No kernel may reach another device: no remote copies, remote signals or barrier semaphores. Data moves between devices by JAX's collectives and lax.ppermute only.
A program may use at most 64 MiB of HBM per device.

```python
import math
import jax
import jax.numpy as jnp
import numpy as np
from jax import lax

MEMBER_TOTAL = 256
BLK = 128
OB = 32
CAPB = 4
SB = 96
BATCHES = 2
SLOTS = 128
NCELLS = 786432
N_SPACE = 64


def with_ends(entries, rng, smallest, top_value):
    place = [jax.random.randint(jax.random.fold_in(rng, axis), (), 0, length) for axis, length in enumerate(entries.shape)]
    longest = entries.shape.index(max(entries.shape))
    beside = place[:longest] + [(place[longest] + 1) % entries.shape[longest]] + place[longest + 1:]
    return entries.at[tuple(place)].set(smallest).at[tuple(beside)].set(top_value)


def steps_of(own_key, extent, pieces, smallest, top_value):
    def one(dim, shards_of):
        draws = jax.random.uniform(jax.random.fold_in(jax.random.fold_in(own_key, 6), dim), (shards_of,), jnp.float32, smallest / len(pieces), top_value / len(pieces))
        return jnp.repeat(jnp.exp(draws), extent[dim] // shards_of).reshape((-1,) + (1,) * (len(extent) - dim - 1))

    gain = one(*pieces[0])
    for cut in pieces[1:]:
        gain = gain * one(*cut)
    return gain


def length_profile(number_of, total, reach, lean):
    loads = [(1 << 20) // math.isqrt(grade ** lean) + 1 for grade in range(2, number_of + 1)]
    surplus, counts = total - reach - (number_of - 1), [1] * (number_of - 1)
    while surplus > 0:
        candidates = [i for i in range(number_of - 1) if counts[i] < reach]
        whole, budget = sum([loads[i] for i in candidates]), surplus
        for i in candidates:
            more = min(reach - counts[i], max(1, budget * loads[i] // whole), surplus)
            counts[i] = counts[i] + more
            surplus = surplus - more
    return np.array([reach] + counts)


def ragged(rng, count, total, most, lean):
    if count == 2:
        one = jax.random.randint(rng, (), max(1, total - most), min(most, total - 1) + 1)
        return jnp.stack([one, total - one])
    lengths = jnp.asarray(length_profile(count, total, most, lean), jnp.int32)
    pairs = (count - 1) // 2
    donor, sink = lengths[1:1 + 2 * pairs:2], lengths[2:2 + 2 * pairs:2]
    margin = jnp.minimum(donor - 1, most - sink)
    moved = jax.random.randint(jax.random.fold_in(rng, 1), (pairs,), 0, 1 << 20) % (margin + 1)
    lengths = lengths.at[1:1 + 2 * pairs:2].set(donor - moved).at[2:2 + 2 * pairs:2].set(sink + moved)
    return lengths[jax.random.permutation(jax.random.fold_in(rng, 2), count)]


def normal_values(rng, dims, deviation, bound, split=(), dtype=jnp.bfloat16):
    values = deviation * jax.random.normal(rng, dims, jnp.float32)
    if split:
        values = values * steps_of(rng, dims, split, -0.22, 0.18)
    return jnp.clip(values, -bound, bound).astype(dtype)


def setup_inputs(seed: int = 0) -> dict:
    arg_keys = jax.random.split(jax.random.key(seed), 8)
    prior_state = normal_values(arg_keys[0], (MEMBER_TOTAL, NCELLS), 1.0, 6.0, ((0, 8), (1, 64)))
    block_counts = jax.vmap(lambda own: ragged(own, N_SPACE, 2 * N_SPACE, CAPB, 2))(jax.random.split(arg_keys[1], BATCHES)).reshape((BATCHES, N_SPACE)).astype(jnp.int32)
    block_index = with_ends(jax.random.randint(arg_keys[2], (BATCHES, N_SPACE * CAPB), 0, SB), jax.random.fold_in(arg_keys[2], 1), 0, SB - 1).astype(jnp.int32)
    gate_operator = normal_values(arg_keys[3], (BATCHES, N_SPACE * CAPB, OB, BLK), BLK ** -0.5, 0.5, ((1, 64),), jnp.float32)
    observed = normal_values(arg_keys[4], (BATCHES, N_SPACE * SLOTS), 1.5, 8.0, ((1, 64),), jnp.float32)
    obs_error = jnp.clip(jnp.exp(math.log(4.0) - 2.7725887 * jax.random.uniform(arg_keys[5], (BATCHES, N_SPACE * SLOTS), jnp.float32) ** steps_of(arg_keys[5], (BATCHES, N_SPACE * SLOTS), ((1, 64),), -0.2, 0.2)), 0.25, 4.0)
    local_mask = with_ends((jax.random.randint(arg_keys[6], (BATCHES, N_SPACE * SB, 5 * CAPB), 0, 2) < 1).astype(jnp.int32), jax.random.fold_in(arg_keys[6], 1), 0, 1)
    return dict(prior_state=prior_state, block_counts=block_counts, block_index=block_index, gate_operator=gate_operator, observed=observed, obs_error=obs_error, local_mask=local_mask)


def reference(prior_state, block_counts, block_index, gate_operator, observed, obs_error, local_mask):
    tile_count = N_SPACE
    largest_value = lax.Precision.HIGHEST
    state_now = prior_state
    tile_ids = jnp.arange(tile_count)[:, None]
    slot_block = jnp.arange(SLOTS) // OB
    for batch_id in range(BATCHES):
        blocks = state_now.reshape(MEMBER_TOTAL, tile_count, SB, BLK)
        slot_blocks = block_index[batch_id].reshape(tile_count, CAPB).astype(jnp.int32)
        picked = blocks[:, tile_ids, slot_blocks, :].astype(jnp.float32)
        operator_blocks = gate_operator[batch_id].reshape(tile_count, CAPB, OB, BLK)
        prior = jnp.einsum('mtcb,tcob->mtco', picked, operator_blocks, precision=largest_value).reshape(MEMBER_TOTAL, tile_count, SLOTS)
        mean_obs = lax.optimization_barrier(jnp.sum(prior, 0)) / MEMBER_TOTAL
        spread = prior - mean_obs
        variance = lax.optimization_barrier(jnp.sum(spread * spread, 0)) / (MEMBER_TOTAL - 1)
        error_now = obs_error[batch_id].reshape(tile_count, SLOTS)
        values_now = observed[batch_id].reshape(tile_count, SLOTS)
        gain_term = 1.0 / (variance + error_now)
        shrink = gain_term / (1.0 + jnp.sqrt(error_now * gain_term))
        live_slot = slot_block[None, :] < block_counts[batch_id][:, None]
        weights = jnp.where(live_slot[None], gain_term * (values_now - mean_obs) - shrink * spread, 0.0)
        packed = jnp.pad(jnp.stack([spread, weights]), ((0, 0), (0, 0), (2, 2), (0, 0)))
        neighbour_blocks = jnp.concatenate([packed[:, :, shift_at:shift_at + tile_count] for shift_at in range(5)], axis=3)
        mask_rows = local_mask[batch_id].reshape(tile_count, SB, 5 * CAPB).astype(jnp.float32)
        state_cells = blocks.astype(jnp.float32)
        member_deviation = state_cells - lax.optimization_barrier(jnp.mean(state_cells, 0))

        def tile_update(inputs):
            tile_deviation, neighbour_spread, neighbour_weights, tile_mask = inputs
            cross_covariance = jnp.einsum('qfi,qx->fix', tile_deviation, neighbour_spread, precision=largest_value) / (MEMBER_TOTAL - 1)
            spread_block_mask = jnp.repeat(tile_mask, OB, axis=1)
            return jnp.einsum('vn,xdn->vxd', neighbour_weights, cross_covariance * spread_block_mask[:, None, :], precision=largest_value)
        increment = lax.map(tile_update, (member_deviation.transpose(1, 0, 2, 3), neighbour_blocks[0].transpose(1, 0, 2), neighbour_blocks[1].transpose(1, 0, 2), mask_rows))
        state_now = (state_cells + increment.transpose(1, 0, 2, 3)).reshape(MEMBER_TOTAL, NCELLS).astype(jnp.bfloat16)
    return state_now
```

```python
import jax
import jax.numpy as jnp
from jax import lax
from jax.experimental import pallas as pl
from jax.experimental.pallas import tpu as pltpu
from jax.sharding import PartitionSpec as P

MEMBERS = 256
BLK = 128
OB = 32
CAPB = 4
SB = 96
SLOTS = 128
BATCHES = 2
ROWS = 48
PACK = 272
F32 = jnp.float32
BF16 = jnp.bfloat16


def two_parts(value):
    high = value.astype(BF16).astype(F32)
    return high, value - high


def dot(a, b, dims):
    return lax.dot_general(a, b, (dims, ((), ())), preferred_element_type=F32)


def observe_kernel(index_ref, gate_ref, state_ref, out_ref, moved_ref, picks, sems, move_sems):
    groups, mem_dev, width = moved_ref.shape
    copies = []
    for k in range(BATCHES):
        for c in range(CAPB):
            n = k * CAPB + c
            start = pl.multiple_of(index_ref[k, c] * BLK, BLK)
            copies.append(
                pltpu.make_async_copy(state_ref.at[:, pl.ds(start, BLK)], picks.at[n], sems.at[n])
            )
    moves = [
        pltpu.make_async_copy(
            state_ref.at[:, pl.ds(g * width, width)], moved_ref.at[g], move_sems.at[g]
        )
        for g in range(groups)
    ]
    for copy in copies + moves:
        copy.start()
    high, low = two_parts(gate_ref[...].reshape(BATCHES * CAPB * OB, BLK))
    for copy in copies:
        copy.wait()
    rows = picks[...].reshape(BATCHES * CAPB * mem_dev, BLK)
    each = dot(rows, high.astype(BF16), ((1,), (1,))) + dot(rows, low.astype(BF16), ((1,), (1,)))
    lane_block = lax.broadcasted_iota(jnp.int32, (mem_dev, BATCHES * SLOTS), 1) // OB
    prior = jnp.zeros((mem_dev, BATCHES * SLOTS), F32)
    for n in range(BATCHES * CAPB):
        prior = jnp.where(lane_block == n, each[n * mem_dev : (n + 1) * mem_dev], prior)
    mean = jnp.sum(prior, 0, keepdims=True) / mem_dev
    mean_high, mean_low = two_parts(mean)
    spare = ROWS - mem_dev
    row = lax.broadcasted_iota(jnp.int32, (spare, BATCHES * SLOTS), 0)
    tail = jnp.where(row == 0, mean_high, jnp.where(row == 1, mean_low, 0.0))
    block = jnp.concatenate([prior - mean, tail], 0).astype(BF16)
    for g in range(groups):
        out_ref[g] = block
    for move in moves:
        move.wait()


def observe(block_index, gate_operator, prior_state, groups):
    mem_dev, cells = prior_state.shape
    return pl.pallas_call(
        observe_kernel,
        in_specs=[
            pl.BlockSpec(memory_space=pltpu.SMEM),
            pl.BlockSpec(memory_space=pltpu.VMEM),
            pl.BlockSpec(memory_space=pl.ANY),
        ],
        out_specs=[pl.BlockSpec(memory_space=pltpu.VMEM), pl.BlockSpec(memory_space=pl.ANY)],
        out_shape=[
            jax.ShapeDtypeStruct((groups, ROWS, BATCHES * SLOTS), BF16),
            jax.ShapeDtypeStruct((groups, mem_dev, cells // groups), BF16),
        ],
        scratch_shapes=[
            pltpu.VMEM((BATCHES * CAPB, mem_dev, BLK), BF16),
            pltpu.SemaphoreType.DMA((BATCHES * CAPB,)),
            pltpu.SemaphoreType.DMA((groups,)),
        ],
        name="observe",
    )(block_index, gate_operator, prior_state)


def members_of(shared_ref, batch_id):
    groups = shared_ref.shape[0]
    mem_dev = MEMBERS // groups
    lanes = slice(batch_id * SLOTS, (batch_id + 1) * SLOTS)
    parts = []
    for g in range(groups):
        block = shared_ref[g, :, lanes].astype(F32)
        parts.append(block[:mem_dev] + (block[mem_dev : mem_dev + 1] + block[mem_dev + 1 : mem_dev + 2]))
    return jnp.concatenate(parts, 0)


def store_packed(out_ref, prior, observed, error_now, live_count):
    mean_obs = jnp.sum(prior, 0, keepdims=True) / MEMBERS
    spread = prior - mean_obs
    variance = jnp.sum(spread * spread, 0, keepdims=True) / (MEMBERS - 1)
    gain = 1.0 / (variance + error_now)
    shrink = gain / (1.0 + jnp.sqrt(error_now * gain))
    live = lax.broadcasted_iota(jnp.int32, (1, SLOTS), 1) // OB < live_count
    level = jnp.where(live, gain * (observed - mean_obs), 0.0)
    slope = jnp.where(live, shrink, 0.0)
    level_high, level_low = two_parts(level)
    slope_high, slope_low = two_parts(slope)
    row = lax.broadcasted_iota(jnp.int32, (PACK - MEMBERS, SLOTS), 0)
    tail = jnp.where(
        row == 0,
        level_high,
        jnp.where(row == 1, level_low, jnp.where(row == 2, slope_high, jnp.where(row == 3, slope_low, 0.0))),
    )
    out_ref[:MEMBERS] = spread.astype(BF16)
    out_ref[MEMBERS:] = tail.astype(BF16)


def first_pack_kernel(counts_ref, shared_ref, observed_ref, error_ref, out_ref):
    store_packed(
        out_ref, members_of(shared_ref, 0), observed_ref[0:1], error_ref[0:1], counts_ref[0, 0]
    )


def window(own_ref, around_ref):
    return [
        (0, own_ref[...]),
        (-1, around_ref[0, 0]),
        (-2, around_ref[0, 1]),
        (1, around_ref[1, 0]),
        (2, around_ref[1, 1]),
    ]


def weights_of(pack):
    tail = pack[MEMBERS:].astype(F32)
    level = tail[0:1] + tail[1:2]
    slope = tail[2:3] + tail[3:4]
    return (level - slope * pack[:MEMBERS].astype(F32)).astype(BF16)


def turned(pack):
    return jnp.transpose(pack[:MEMBERS].astype(F32)).astype(BF16)


def second_pack_kernel(
    counts_ref, index_ref, mask_ref, shared_ref, own_ref, around_ref, observed_ref, error_ref, out_ref
):
    prior = members_of(shared_ref, 1)
    deviation = (prior - jnp.sum(prior, 0, keepdims=True) / MEMBERS).astype(BF16)
    lane_block = lax.broadcasted_iota(jnp.int32, (1, SLOTS), 1) // OB
    total = prior
    for offset, pack in window(own_ref, around_ref):
        covariance = dot(turned(pack), deviation, ((1,), (0,)))
        kept = []
        for c in range(CAPB):
            column = (offset + 2) * CAPB + c
            keep = jnp.zeros((1, SLOTS), F32)
            for b in range(CAPB):
                flag = mask_ref[0, index_ref[1, b], column].astype(F32) * (1.0 / (MEMBERS - 1))
                keep = jnp.where(lane_block == b, flag, keep)
            kept.append(covariance[c * OB : (c + 1) * OB] * keep)
        kept = jnp.concatenate(kept, 0).astype(BF16)
        total = total + dot(weights_of(pack), kept, ((1,), (0,)))
    store_packed(out_ref, total, observed_ref[1:2], error_ref[1:2], counts_ref[1, 0])


def update_kernel(batch_id, place_ref, mask_ref, own_ref, around_ref, state_ref, out_ref, turned_ref, weights_ref):
    tiles = window(own_ref, around_ref)
    for n, (_, pack) in enumerate(tiles):
        turned_ref[n * SLOTS : (n + 1) * SLOTS] = turned(pack)
        weights_ref[:, n * SLOTS : (n + 1) * SLOTS] = weights_of(pack)
    cells = state_ref.shape[1]
    first = place_ref[0] * (cells // BLK)
    step = 2 * BLK
    for at in range(0, cells, step):
        values = state_ref[:, at : at + step].astype(F32)
        mean = jnp.sum(values, 0, keepdims=True) / MEMBERS
        covariance = dot(turned_ref[...], (values - mean).astype(BF16), ((1,), (0,)))
        rows = []
        for n, (offset, _) in enumerate(tiles):
            for c in range(CAPB):
                row = covariance[n * SLOTS + c * OB : n * SLOTS + (c + 1) * OB]
                halves = []
                for h in range(2):
                    block = first + (at // BLK + h)
                    flag = mask_ref[batch_id, block, (offset + 2) * CAPB + c].astype(F32) * (
                        1.0 / (MEMBERS - 1)
                    )
                    halves.append(row[:, h * BLK : (h + 1) * BLK] * flag)
                rows.append(jnp.concatenate(halves, 1))
        kept = jnp.concatenate(rows, 0).astype(BF16)
        increment = dot(weights_ref[...], kept, ((1,), (0,)))
        out_ref[:, at : at + step] = (values + increment).astype(BF16)


VM = pl.BlockSpec(memory_space=pltpu.VMEM)
SM = pl.BlockSpec(memory_space=pltpu.SMEM)


def first_pack(counts, shared, observed, errors):
    return pl.pallas_call(
        first_pack_kernel,
        in_specs=[SM, VM, VM, VM],
        out_specs=VM,
        out_shape=jax.ShapeDtypeStruct((PACK, SLOTS), BF16),
        name="first_pack",
    )(counts, shared, observed, errors)


def second_pack(counts, index, mask, shared, own, around, observed, errors):
    return pl.pallas_call(
        second_pack_kernel,
        in_specs=[SM, SM, SM, VM, VM, VM, VM, VM],
        out_specs=VM,
        out_shape=jax.ShapeDtypeStruct((PACK, SLOTS), BF16),
        name="second_pack",
    )(counts, index, mask, shared, own, around, observed, errors)


def update(batch_id, place, mask, own, around, state):
    return pl.pallas_call(
        lambda *refs: update_kernel(batch_id, *refs),
        in_specs=[SM, SM, VM, VM, VM],
        out_specs=VM,
        out_shape=jax.ShapeDtypeStruct(state.shape, BF16),
        scratch_shapes=[pltpu.VMEM((5 * SLOTS, MEMBERS), BF16), pltpu.VMEM((MEMBERS, 5 * SLOTS), BF16)],
        compiler_params=pltpu.CompilerParams(vmem_limit_bytes=32 * 1024 * 1024),
        name="update",
    )(place, mask, own, around, state)


def shared_around(pack):
    tiles, groups = lax.axis_size("space"), lax.axis_size("mem")
    received = []
    for offset in (1, 2):
        pairs = []
        for tile in range(tiles):
            for m in range(groups):
                target = tile + offset if m % 2 == 0 else tile - offset
                if 0 <= target < tiles:
                    pairs.append((tile * groups + m, target * groups + m))
        received.append(lax.ppermute(pack, ("space", "mem"), pairs))
    chips = [[2 * chip, 2 * chip + 1] for chip in range(groups // 2)]
    return lax.all_gather(jnp.stack(received), "mem", axis=0, axis_index_groups=chips)


def per_device(prior_state, block_counts, block_index, gate_operator, observed, obs_error, local_mask):
    groups = lax.axis_size("mem")
    mem_dev, cells = prior_state.shape
    place = lax.axis_index("mem").astype(jnp.int32).reshape(1)
    own_block, moved = observe(block_index, gate_operator, prior_state, groups)
    shared = lax.all_to_all(own_block, "mem", split_axis=0, concat_axis=0, tiled=True)
    state = lax.all_to_all(moved, "mem", split_axis=0, concat_axis=0, tiled=True)
    state = state.reshape(MEMBERS, cells // groups)
    pack = first_pack(block_counts, shared, observed, obs_error)
    around = shared_around(pack)
    next_pack = second_pack(
        block_counts, block_index, local_mask, shared, pack, around, observed, obs_error
    )
    state = update(0, place, local_mask, pack, around, state)
    next_around = shared_around(next_pack)
    state = update(1, place, local_mask, next_pack, next_around, state)
    parts = lax.all_to_all(
        state.reshape(groups, mem_dev, cells // groups), "mem", split_axis=0, concat_axis=0, tiled=True
    )
    return parts.transpose(1, 0, 2).reshape(mem_dev, cells)


def solution(mesh):
    placed = (
        P("mem", "space"),
        P(None, "space"),
        P(None, "space"),
        P(None, "space", None, None),
        P(None, "space"),
        P(None, "space"),
        P(None, "space", None),
    )
    return jax.shard_map(
        per_device, mesh=mesh, in_specs=placed, out_specs=P("mem", "space"), check_vma=False
    )
```

```python
import jax
import jax.numpy as jnp
from jax import lax
from jax.experimental import pallas as pl
from jax.experimental.pallas import tpu as pltpu
from jax.sharding import PartitionSpec as P

MEMBERS = 256
BLK = 128
OB = 32
CAPB = 4
SB = 96
SLOTS = 128
BATCHES = 2
ROWS = 48
PACK = 272
F32 = jnp.float32
BF16 = jnp.bfloat16


def two_parts(value):
    high = value.astype(BF16).astype(F32)
    return high, value - high


def dot(a, b, dims):
    return lax.dot_general(a, b, (dims, ((), ())), preferred_element_type=F32)


def observe_kernel(index_ref, gate_ref, state_ref, out_ref, moved_ref):
    groups, mem_dev, width = moved_ref.shape
    high, low = two_parts(gate_ref[...].reshape(BATCHES * CAPB * OB, BLK))
    picks = []
    for k in range(BATCHES):
        for c in range(CAPB):
            start = pl.multiple_of(index_ref[k, c] * BLK, BLK)
            picks.append(state_ref[:, pl.ds(start, BLK)])
    rows = jnp.concatenate(picks, 0)
    each = dot(rows, high.astype(BF16), ((1,), (1,))) + dot(rows, low.astype(BF16), ((1,), (1,)))
    lane_block = lax.broadcasted_iota(jnp.int32, (mem_dev, BATCHES * SLOTS), 1) // OB
    prior = jnp.zeros((mem_dev, BATCHES * SLOTS), F32)
    for n in range(BATCHES * CAPB):
        prior = jnp.where(lane_block == n, each[n * mem_dev : (n + 1) * mem_dev], prior)
    mean = jnp.sum(prior, 0, keepdims=True) / mem_dev
    mean_high, mean_low = two_parts(mean)
    spare = ROWS - mem_dev
    row = lax.broadcasted_iota(jnp.int32, (spare, BATCHES * SLOTS), 0)
    tail = jnp.where(row == 0, mean_high, jnp.where(row == 1, mean_low, 0.0))
    block = jnp.concatenate([prior - mean, tail], 0).astype(BF16)
    for g in range(groups):
        out_ref[g] = block
        moved_ref[g] = state_ref[:, g * width : (g + 1) * width]


def members_of(shared_ref, batch_id):
    groups = shared_ref.shape[0]
    mem_dev = MEMBERS // groups
    lanes = slice(batch_id * SLOTS, (batch_id + 1) * SLOTS)
    parts = []
    for g in range(groups):
        block = shared_ref[g, :, lanes].astype(F32)
        parts.append(block[:mem_dev] + (block[mem_dev : mem_dev + 1] + block[mem_dev + 1 : mem_dev + 2]))
    return jnp.concatenate(parts, 0)


def store_packed(out_ref, prior, observed, error_now, live_count):
    mean_obs = jnp.sum(prior, 0, keepdims=True) / MEMBERS
    spread = prior - mean_obs
    variance = jnp.sum(spread * spread, 0, keepdims=True) / (MEMBERS - 1)
    gain = 1.0 / (variance + error_now)
    shrink = gain / (1.0 + jnp.sqrt(error_now * gain))
    live = lax.broadcasted_iota(jnp.int32, (1, SLOTS), 1) // OB < live_count
    scale = jnp.sqrt(shrink / (MEMBERS - 1))
    level = jnp.where(live, gain * (observed - mean_obs) / (scale * (MEMBERS - 1)), 0.0)
    scaled = (spread * jnp.where(live, scale, 0.0)).astype(BF16)
    total = jnp.sum(scaled.astype(F32), 0, keepdims=True)
    level_high, level_low = two_parts(level)
    total_high, total_low = two_parts(total)
    row = lax.broadcasted_iota(jnp.int32, (PACK - MEMBERS, SLOTS), 0)
    tail = jnp.where(
        row == 0,
        level_high,
        jnp.where(row == 1, level_low, jnp.where(row == 2, total_high, jnp.where(row == 3, total_low, 0.0))),
    )
    out_ref[:MEMBERS] = scaled
    out_ref[MEMBERS:] = tail.astype(BF16)


def first_pack_kernel(counts_ref, shared_ref, observed_ref, error_ref, out_ref):
    store_packed(
        out_ref, members_of(shared_ref, 0), observed_ref[0:1], error_ref[0:1], counts_ref[0:1, 0:1]
    )


def window(own_ref, around_ref):
    return [
        (0, own_ref),
        (-1, around_ref.at[0, 0]),
        (-2, around_ref.at[0, 1]),
        (1, around_ref.at[1, 0]),
        (2, around_ref.at[1, 1]),
    ]


def turned(pack):
    return jnp.transpose(pack[:MEMBERS].astype(F32)).astype(BF16)


def column_of(pack, row):
    value = pack[row : row + 1].astype(F32) + pack[row + 1 : row + 2].astype(F32)
    return jnp.transpose(jnp.broadcast_to(value, (SLOTS, SLOTS)))


def applied(change):
    return (change[MEMBERS : MEMBERS + 1] + change[MEMBERS + 1 : MEMBERS + 2]) - change[:MEMBERS]


def second_pack_kernel(
    counts_ref, index_ref, mask_ref, shared_ref, own_ref, around_ref, observed_ref, error_ref, out_ref
):
    prior = members_of(shared_ref, 1)
    high, low = two_parts(prior - jnp.sum(prior, 0, keepdims=True) / MEMBERS)
    deviation = jnp.concatenate([high, low], 1).astype(BF16)
    lane_block = lax.broadcasted_iota(jnp.int32, (1, SLOTS), 1) // OB
    change = jnp.zeros((PACK, 2 * SLOTS), F32)
    for offset, pack_ref in window(own_ref, around_ref):
        pack = pack_ref[...]
        covariance = dot(turned(pack), deviation, ((1,), (0,)))
        covariance = covariance[:, :SLOTS] + covariance[:, SLOTS:]
        kept = []
        for c in range(CAPB):
            column = (offset + 2) * CAPB + c
            keep = jnp.zeros((1, SLOTS), F32)
            for b in range(CAPB):
                flag = mask_ref[0, index_ref[1, b], column].astype(F32)
                keep = jnp.where(lane_block == b, flag, keep)
            kept.append(covariance[c * OB : (c + 1) * OB] * keep)
        high, low = two_parts(jnp.concatenate(kept, 0))
        change = change + dot(pack, jnp.concatenate([high, low], 1).astype(BF16), ((1,), (0,)))
    prior = prior + applied(change[:, :SLOTS] + change[:, SLOTS:])
    store_packed(out_ref, prior, observed_ref[1:2], error_ref[1:2], counts_ref[1:2, 0:1])


def update_kernel(
    batch_id, place_ref, mask_ref, own_ref, around_ref, state_ref, out_ref,
    turned_ref, packs_ref, total_ref, kept_ref,
):
    tiles = window(own_ref, around_ref)
    for n, (_, pack_ref) in enumerate(tiles):
        span = slice(n * SLOTS, (n + 1) * SLOTS)
        pack = pack_ref[...]
        turned_ref[span] = turned(pack)
        packs_ref[:, 2 * n * SLOTS : (2 * n + 1) * SLOTS] = pack
        packs_ref[:, (2 * n + 1) * SLOTS : (2 * n + 2) * SLOTS] = pack
        total_ref[span] = column_of(pack, MEMBERS + 2)
    cells = state_ref.shape[1]
    first = place_ref[0] * (cells // BLK)
    step = 2 * BLK
    for at in range(0, cells, step):
        buffer = at // step % 2
        values = state_ref[:, at : at + step]
        mean = jnp.sum(values.astype(F32), 0, keepdims=True) / MEMBERS
        covariance = dot(turned_ref[...], values, ((1,), (0,)))
        for n, (offset, _) in enumerate(tiles):
            for c in range(CAPB):
                span = slice(n * SLOTS + c * OB, n * SLOTS + (c + 1) * OB)
                total = total_ref[span]
                row = 2 * n * SLOTS + c * OB
                for h in range(2):
                    lanes = slice(h * BLK, (h + 1) * BLK)
                    block = first + (at // BLK + h)
                    flag = mask_ref[batch_id, block, (offset + 2) * CAPB + c].astype(F32)
                    kept = (covariance[span, lanes] - total * mean[:, lanes]) * flag
                    high, low = two_parts(kept)
                    kept_ref[buffer, row : row + OB, lanes] = high.astype(BF16)
                    kept_ref[buffer, row + SLOTS : row + SLOTS + OB, lanes] = low.astype(BF16)
        change = dot(packs_ref[...], kept_ref[buffer], ((1,), (0,)))
        out_ref[:, at : at + step] = (values.astype(F32) + applied(change)).astype(BF16)


PARAMS = pltpu.CompilerParams(vmem_limit_bytes=32 * 1024 * 1024)
VM = pl.BlockSpec(memory_space=pltpu.VMEM)
SM = pl.BlockSpec(memory_space=pltpu.SMEM)


def observe(block_index, gate_operator, prior_state, groups):
    mem_dev, cells = prior_state.shape
    return pl.pallas_call(
        observe_kernel,
        in_specs=[SM, VM, VM],
        out_specs=[VM, VM],
        out_shape=[
            jax.ShapeDtypeStruct((groups, ROWS, BATCHES * SLOTS), BF16),
            jax.ShapeDtypeStruct((groups, mem_dev, cells // groups), BF16),
        ],
        compiler_params=PARAMS,
        name="observe",
    )(block_index, gate_operator, prior_state)


def first_pack(counts, shared, observed, errors):
    return pl.pallas_call(
        first_pack_kernel,
        in_specs=[VM, VM, VM, VM],
        out_specs=VM,
        out_shape=jax.ShapeDtypeStruct((PACK, SLOTS), BF16),
        compiler_params=PARAMS,
        name="first_pack",
    )(counts, shared, observed, errors)


def second_pack(counts, index, mask, shared, own, around, observed, errors):
    return pl.pallas_call(
        second_pack_kernel,
        in_specs=[VM, SM, SM, VM, VM, VM, VM, VM],
        out_specs=VM,
        out_shape=jax.ShapeDtypeStruct((PACK, SLOTS), BF16),
        compiler_params=PARAMS,
        name="second_pack",
    )(counts, index, mask, shared, own, around, observed, errors)


def update(batch_id, place, mask, own, around, state):
    return pl.pallas_call(
        lambda *refs: update_kernel(batch_id, *refs),
        in_specs=[SM, SM, VM, VM, VM],
        out_specs=VM,
        out_shape=jax.ShapeDtypeStruct(state.shape, BF16),
        scratch_shapes=[
            pltpu.VMEM((5 * SLOTS, MEMBERS), BF16),
            pltpu.VMEM((PACK, 10 * SLOTS), BF16),
            pltpu.VMEM((5 * SLOTS, BLK), F32),
            pltpu.VMEM((2, 10 * SLOTS, 2 * BLK), BF16),
        ],
        compiler_params=PARAMS,
        name="update",
    )(place, mask, own, around, state)


def passed_around(pack):
    tiles, groups = lax.axis_size("space"), lax.axis_size("mem")
    received = []
    for offset in (1, 2):
        pairs = []
        for tile in range(tiles):
            for m in range(groups):
                target = tile + offset if m % 2 == 0 else tile - offset
                if 0 <= target < tiles:
                    pairs.append((tile * groups + m, target * groups + m))
        received.append(lax.ppermute(pack, ("space", "mem"), pairs))
    return jnp.stack(received)


def chip_shared(received):
    groups = lax.axis_size("mem")
    chips = [[2 * chip, 2 * chip + 1] for chip in range(groups // 2)]
    return lax.all_gather(received, "mem", axis=0, axis_index_groups=chips)


def per_device(prior_state, block_counts, block_index, gate_operator, observed, obs_error, local_mask):
    groups = lax.axis_size("mem")
    mem_dev, cells = prior_state.shape
    place = lax.axis_index("mem").astype(jnp.int32).reshape(1)
    own_block, moved = observe(block_index, gate_operator, prior_state, groups)
    shared = lax.all_to_all(own_block, "mem", split_axis=0, concat_axis=0, tiled=True)
    pack = first_pack(block_counts, shared, observed, obs_error)
    received = passed_around(pack)
    moved, pack = lax.optimization_barrier((moved, pack))
    state = lax.all_to_all(moved, "mem", split_axis=0, concat_axis=0, tiled=True)
    state = state.reshape(MEMBERS, cells // groups)
    around = chip_shared(received)
    around, state = lax.optimization_barrier((around, state))
    next_pack = second_pack(
        block_counts, block_index, local_mask, shared, pack, around, observed, obs_error
    )
    received = passed_around(next_pack)
    state = update(0, place, local_mask, pack, around, state)
    received, state = lax.optimization_barrier((received, state))
    next_around = chip_shared(received)
    state = update(1, place, local_mask, next_pack, next_around, state)
    parts = lax.all_to_all(
        state.reshape(groups, mem_dev, cells // groups), "mem", split_axis=0, concat_axis=0, tiled=True
    )
    return parts.transpose(1, 0, 2).reshape(mem_dev, cells)


def solution(mesh):
    placed = (
        P("mem", "space"),
        P(None, "space"),
        P(None, "space"),
        P(None, "space", None, None),
        P(None, "space"),
        P(None, "space"),
        P(None, "space", None),
    )
    return jax.shard_map(
        per_device, mesh=mesh, in_specs=placed, out_specs=P("mem", "space"), check_vma=False
    )
```

```python
import jax
import jax.numpy as jnp
from jax import lax
from jax.experimental import pallas as pl
from jax.experimental.pallas import tpu as pltpu
from jax.sharding import PartitionSpec as P

MEMBERS = 256
BLK = 128
OB = 32
CAPB = 4
SB = 96
SLOTS = 128
BATCHES = 2
ROWS = 48
PACK = 272
F32 = jnp.float32
BF16 = jnp.bfloat16


def two_parts(value):
    high = value.astype(BF16).astype(F32)
    return high, value - high


def dot(a, b, dims):
    return lax.dot_general(a, b, (dims, ((), ())), preferred_element_type=F32)


def observe_kernel(index_hbm, gate_ref, state_ref, out_ref, index_ref, gate, picks, index_sem, gate_sem, sems):
    mem_dev = state_ref.shape[0]
    index_copy = pltpu.make_async_copy(index_hbm, index_ref, index_sem)
    index_copy.start()
    gate_copy = pltpu.make_async_copy(gate_ref, gate, gate_sem)
    gate_copy.start()
    index_copy.wait()
    copies = []
    for k in range(BATCHES):
        for c in range(CAPB):
            n = k * CAPB + c
            start = pl.multiple_of(index_ref[k, c] * BLK, BLK)
            copies.append(
                pltpu.make_async_copy(state_ref.at[:, pl.ds(start, BLK)], picks.at[n], sems.at[n])
            )
    for copy in copies:
        copy.start()
    gate_copy.wait()
    high, low = two_parts(gate[...].reshape(BATCHES * CAPB * OB, BLK))
    for copy in copies:
        copy.wait()
    rows = picks[...].reshape(BATCHES * CAPB * mem_dev, BLK)
    each = dot(rows, high.astype(BF16), ((1,), (1,))) + dot(rows, low.astype(BF16), ((1,), (1,)))
    lane_block = lax.broadcasted_iota(jnp.int32, (mem_dev, BATCHES * SLOTS), 1) // OB
    prior = jnp.zeros((mem_dev, BATCHES * SLOTS), F32)
    for n in range(BATCHES * CAPB):
        prior = jnp.where(lane_block == n, each[n * mem_dev : (n + 1) * mem_dev], prior)
    mean = jnp.sum(prior, 0, keepdims=True) / mem_dev
    mean_high, mean_low = two_parts(mean)
    row = lax.broadcasted_iota(jnp.int32, (ROWS - mem_dev, BATCHES * SLOTS), 0)
    tail = jnp.where(row == 0, mean_high, jnp.where(row == 1, mean_low, 0.0))
    block = jnp.concatenate([prior - mean, tail], 0).astype(BF16)
    for g in range(out_ref.shape[0]):
        out_ref[g] = block


def gather_small_kernel(place_ref, counts_ref, index_ref, mask_ref, observed_ref, error_ref, between_ref, own_ref, slots_ref):
    columns, _, blocks = mask_ref.shape
    lane_block = lax.broadcasted_iota(jnp.int32, (1, SLOTS), 1) // OB
    wanted = jnp.zeros((1, SLOTS), jnp.int32)
    for b in range(CAPB):
        wanted = jnp.where(lane_block == b, index_ref[1, b], wanted)
    chosen = (lax.broadcasted_iota(jnp.int32, (blocks, SLOTS), 0) == wanted).astype(F32).astype(BF16)
    mask = mask_ref[...].astype(F32).astype(BF16)
    between_ref[...] = dot(mask[:, 0], chosen, ((1,), (0,)))
    rows = own_ref.shape[1]
    row = lax.broadcasted_iota(jnp.int32, (rows, blocks), 0) + place_ref[0] * rows
    mine = (lax.broadcasted_iota(jnp.int32, (rows, blocks), 1) == row).astype(F32).astype(BF16)
    for k in range(BATCHES):
        own_ref[k] = dot(mine, mask[:, k], ((1,), (1,)))
        slots_ref[3 * k : 3 * k + 1] = observed_ref[k : k + 1]
        slots_ref[3 * k + 1 : 3 * k + 2] = error_ref[k : k + 1]
        slots_ref[3 * k + 2 : 3 * k + 3] = (lane_block < counts_ref[k, 0]).astype(F32)


def members_of(shared_ref, batch_id):
    groups = shared_ref.shape[0]
    mem_dev = MEMBERS // groups
    lanes = slice(batch_id * SLOTS, (batch_id + 1) * SLOTS)
    parts = []
    for g in range(groups):
        block = shared_ref[g, :, lanes].astype(F32)
        parts.append(block[:mem_dev] + (block[mem_dev : mem_dev + 1] + block[mem_dev + 1 : mem_dev + 2]))
    return jnp.concatenate(parts, 0)


def store_packed(out_ref, prior, slots):
    observed, error_now, live = slots[0:1], slots[1:2], slots[2:3] > 0.5
    mean_obs = jnp.sum(prior, 0, keepdims=True) / MEMBERS
    spread = prior - mean_obs
    variance = jnp.sum(spread * spread, 0, keepdims=True) / (MEMBERS - 1)
    gain = 1.0 / (variance + error_now)
    shrink = gain / (1.0 + jnp.sqrt(error_now * gain))
    scale = jnp.sqrt(shrink / (MEMBERS - 1))
    level = jnp.where(live, gain * (observed - mean_obs) / (scale * (MEMBERS - 1)), 0.0)
    scaled = (spread * jnp.where(live, scale, 0.0)).astype(BF16)
    total = jnp.sum(scaled.astype(F32), 0, keepdims=True)
    level_high, level_low = two_parts(level)
    total_high, total_low = two_parts(total)
    row = lax.broadcasted_iota(jnp.int32, (PACK - MEMBERS, SLOTS), 0)
    tail = jnp.where(
        row == 0,
        level_high,
        jnp.where(row == 1, level_low, jnp.where(row == 2, total_high, jnp.where(row == 3, total_low, 0.0))),
    )
    out_ref[:MEMBERS] = scaled
    out_ref[MEMBERS:] = tail.astype(BF16)


def first_pack_kernel(shared_ref, slots_ref, out_ref):
    store_packed(out_ref, members_of(shared_ref, 0), slots_ref[0:3])


def window(own_ref, around_ref):
    return [
        (0, own_ref),
        (-1, around_ref.at[0, 0]),
        (-2, around_ref.at[0, 1]),
        (1, around_ref.at[1, 0]),
        (2, around_ref.at[1, 1]),
    ]


def turned(pack):
    return jnp.transpose(pack[:MEMBERS].astype(F32)).astype(BF16)


def column_of(pack, row):
    value = pack[row : row + 1].astype(F32) + pack[row + 1 : row + 2].astype(F32)
    return jnp.transpose(jnp.broadcast_to(value, (SLOTS, SLOTS)))


def applied(change):
    return (change[MEMBERS : MEMBERS + 1] + change[MEMBERS + 1 : MEMBERS + 2]) - change[:MEMBERS]


def second_pack_kernel(flags_ref, shared_ref, own_ref, around_ref, slots_ref, out_ref):
    prior = members_of(shared_ref, 1)
    high, low = two_parts(prior - jnp.sum(prior, 0, keepdims=True) / MEMBERS)
    deviation = jnp.concatenate([high, low], 1).astype(BF16)
    change = jnp.zeros((PACK, 2 * SLOTS), F32)
    for offset, pack_ref in window(own_ref, around_ref):
        pack = pack_ref[...]
        covariance = dot(turned(pack), deviation, ((1,), (0,)))
        covariance = covariance[:, :SLOTS] + covariance[:, SLOTS:]
        kept = []
        for c in range(CAPB):
            column = (offset + 2) * CAPB + c
            kept.append(covariance[c * OB : (c + 1) * OB] * flags_ref[column : column + 1])
        high, low = two_parts(jnp.concatenate(kept, 0))
        change = change + dot(pack, jnp.concatenate([high, low], 1).astype(BF16), ((1,), (0,)))
    prior = prior + applied(change[:, :SLOTS] + change[:, SLOTS:])
    store_packed(out_ref, prior, slots_ref[3:6])


def update_kernel(
    batch_id, flags_ref, own_ref, around_ref, state_ref, out_ref,
    turned_ref, packs_ref, total_ref, kept_ref,
):
    tiles = window(own_ref, around_ref)
    for n, (_, pack_ref) in enumerate(tiles):
        span = slice(n * SLOTS, (n + 1) * SLOTS)
        pack = pack_ref[...]
        turned_ref[span] = turned(pack)
        packs_ref[:, 2 * n * SLOTS : (2 * n + 1) * SLOTS] = pack
        packs_ref[:, (2 * n + 1) * SLOTS : (2 * n + 2) * SLOTS] = pack
        total_ref[span] = column_of(pack, MEMBERS + 2)
    cells = state_ref.shape[1]
    step = 2 * BLK
    for at in range(0, cells, step):
        buffer = at // step % 2
        values = state_ref[:, at : at + step]
        mean = jnp.sum(values.astype(F32), 0, keepdims=True) / MEMBERS
        covariance = dot(turned_ref[...], values, ((1,), (0,)))
        for n, (offset, _) in enumerate(tiles):
            for c in range(CAPB):
                span = slice(n * SLOTS + c * OB, n * SLOTS + (c + 1) * OB)
                total = total_ref[span]
                row = 2 * n * SLOTS + c * OB
                for h in range(2):
                    lanes = slice(h * BLK, (h + 1) * BLK)
                    flag = flags_ref[batch_id, at // BLK + h, (offset + 2) * CAPB + c]
                    kept = (covariance[span, lanes] - total * mean[:, lanes]) * flag
                    high, low = two_parts(kept)
                    kept_ref[buffer, row : row + OB, lanes] = high.astype(BF16)
                    kept_ref[buffer, row + SLOTS : row + SLOTS + OB, lanes] = low.astype(BF16)
        change = dot(packs_ref[...], kept_ref[buffer], ((1,), (0,)))
        out_ref[:, at : at + step] = (values.astype(F32) + applied(change)).astype(BF16)


PARAMS = pltpu.CompilerParams(vmem_limit_bytes=32 * 1024 * 1024)
VM = pl.BlockSpec(memory_space=pltpu.VMEM)
SM = pl.BlockSpec(memory_space=pltpu.SMEM)


def observe(block_index, gate_operator, prior_state, groups):
    mem_dev = prior_state.shape[0]
    anywhere = pl.BlockSpec(memory_space=pltpu.HBM)
    return pl.pallas_call(
        observe_kernel,
        in_specs=[anywhere, anywhere, anywhere],
        out_specs=VM,
        out_shape=jax.ShapeDtypeStruct((groups, ROWS, BATCHES * SLOTS), BF16),
        scratch_shapes=[
            pltpu.SMEM(block_index.shape, jnp.int32),
            pltpu.VMEM(gate_operator.shape, F32),
            pltpu.VMEM((BATCHES * CAPB, mem_dev, BLK), BF16),
            pltpu.SemaphoreType.DMA(()),
            pltpu.SemaphoreType.DMA(()),
            pltpu.SemaphoreType.DMA((BATCHES * CAPB,)),
        ],
        compiler_params=pltpu.CompilerParams(vmem_limit_bytes=64 * 1024 * 1024 - 65536),
        name="observe",
    )(block_index, gate_operator, prior_state)


def gather_small(place, counts, index, local_mask, observed, errors, blocks):
    columns = local_mask.shape[2]
    return pl.pallas_call(
        gather_small_kernel,
        in_specs=[SM, SM, SM, VM, VM, VM],
        out_specs=[VM, VM, VM],
        out_shape=[
            jax.ShapeDtypeStruct((columns, SLOTS), F32),
            jax.ShapeDtypeStruct((BATCHES, blocks, columns), F32),
            jax.ShapeDtypeStruct((3 * BATCHES, SLOTS), F32),
        ],
        compiler_params=PARAMS,
        name="gather_small",
    )(place, counts, index, local_mask.transpose(2, 0, 1), observed, errors)


def first_pack(shared, slots):
    return pl.pallas_call(
        first_pack_kernel,
        in_specs=[VM, VM],
        out_specs=VM,
        out_shape=jax.ShapeDtypeStruct((PACK, SLOTS), BF16),
        compiler_params=PARAMS,
        name="first_pack",
    )(shared, slots)


def second_pack(flags, shared, own, around, slots):
    return pl.pallas_call(
        second_pack_kernel,
        in_specs=[VM, VM, VM, VM, VM],
        out_specs=VM,
        out_shape=jax.ShapeDtypeStruct((PACK, SLOTS), BF16),
        compiler_params=PARAMS,
        name="second_pack",
    )(flags, shared, own, around, slots)


def update(batch_id, flags, own, around, state):
    return pl.pallas_call(
        lambda *refs: update_kernel(batch_id, *refs),
        in_specs=[SM, VM, VM, VM],
        out_specs=VM,
        out_shape=jax.ShapeDtypeStruct(state.shape, BF16),
        scratch_shapes=[
            pltpu.VMEM((5 * SLOTS, MEMBERS), BF16),
            pltpu.VMEM((PACK, 10 * SLOTS), BF16),
            pltpu.VMEM((5 * SLOTS, BLK), F32),
            pltpu.VMEM((2, 10 * SLOTS, 2 * BLK), BF16),
        ],
        compiler_params=PARAMS,
        name="update",
    )(flags, own, around, state)


def passed_around(pack):
    tiles, groups = lax.axis_size("space"), lax.axis_size("mem")
    received = []
    for offset in (1, 2):
        pairs = []
        for tile in range(tiles):
            for m in range(groups):
                target = tile + offset if m % 2 == 0 else tile - offset
                if 0 <= target < tiles:
                    pairs.append((tile * groups + m, target * groups + m))
        received.append(lax.ppermute(pack, ("space", "mem"), pairs))
    return jnp.stack(received)


def chip_shared(received):
    groups = lax.axis_size("mem")
    chips = [[2 * chip, 2 * chip + 1] for chip in range(groups // 2)]
    return lax.all_gather(received, "mem", axis=0, axis_index_groups=chips)


def per_device(prior_state, block_counts, block_index, gate_operator, observed, obs_error, local_mask):
    groups = lax.axis_size("mem")
    mem_dev, cells = prior_state.shape
    own_block = observe(block_index, gate_operator, prior_state, groups)
    shared = lax.all_to_all(own_block, "mem", split_axis=0, concat_axis=0, tiled=True)
    prior_state, local_mask, own_block = lax.optimization_barrier((prior_state, local_mask, own_block))
    moved = prior_state.reshape(mem_dev, groups, cells // groups).transpose(1, 0, 2)
    place = lax.axis_index("mem").astype(jnp.int32).reshape(1)
    between, flags, slots = gather_small(
        place, block_counts, block_index, local_mask, observed, obs_error, SB // groups
    )
    moved, between, flags, slots = lax.optimization_barrier((moved, between, flags, slots))
    state = lax.all_to_all(moved, "mem", split_axis=0, concat_axis=0, tiled=True)
    state = state.reshape(MEMBERS, cells // groups)
    pack = first_pack(shared, slots)
    around = chip_shared(passed_around(pack))
    next_pack = second_pack(between, shared, pack, around, slots)
    next_pack, state = lax.optimization_barrier((next_pack, state))
    received = passed_around(next_pack)
    state = update(0, flags, pack, around, state)
    received, state = lax.optimization_barrier((received, state))
    next_around = chip_shared(received)
    state = update(1, flags, next_pack, next_around, state)
    parts = lax.all_to_all(
        state.reshape(groups, mem_dev, cells // groups), "mem", split_axis=0, concat_axis=0, tiled=True
    )
    return parts.transpose(1, 0, 2).reshape(mem_dev, cells)


def solution(mesh):
    placed = (
        P("mem", "space"),
        P(None, "space"),
        P(None, "space"),
        P(None, "space", None, None),
        P(None, "space"),
        P(None, "space"),
        P(None, "space", None),
    )
    return jax.shard_map(
        per_device, mesh=mesh, in_specs=placed, out_specs=P("mem", "space"), check_vma=False
    )
```

```python
import jax
import jax.numpy as jnp
from jax import lax
from jax.experimental import pallas as pl
from jax.experimental.pallas import tpu as pltpu
from jax.sharding import PartitionSpec as P

MEMBERS = 256
BLK = 128
OB = 32
CAPB = 4
SB = 96
SLOTS = 128
BATCHES = 2
ROWS = 48
PACK = 272
F32 = jnp.float32
BF16 = jnp.bfloat16


def two_parts(value):
    high = value.astype(BF16).astype(F32)
    return high, value - high


def dot(a, b, dims):
    return lax.dot_general(a, b, (dims, ((), ())), preferred_element_type=F32)


def observe_kernel(index_hbm, gate_ref, state_ref, out_ref, index_ref, gate, picks, index_sem, gate_sem, sems):
    mem_dev = state_ref.shape[0]
    index_copy = pltpu.make_async_copy(index_hbm, index_ref, index_sem)
    index_copy.start()
    gate_copy = pltpu.make_async_copy(gate_ref, gate, gate_sem)
    gate_copy.start()
    index_copy.wait()
    copies = []
    for k in range(BATCHES):
        for c in range(CAPB):
            n = k * CAPB + c
            start = pl.multiple_of(index_ref[k, c] * BLK, BLK)
            copies.append(
                pltpu.make_async_copy(state_ref.at[:, pl.ds(start, BLK)], picks.at[n], sems.at[n])
            )
    for copy in copies:
        copy.start()
    gate_copy.wait()
    high, low = two_parts(gate[...].reshape(BATCHES * CAPB * OB, BLK))
    for copy in copies:
        copy.wait()
    rows = picks[...].reshape(BATCHES * CAPB * mem_dev, BLK)
    each = dot(rows, high.astype(BF16), ((1,), (1,))) + dot(rows, low.astype(BF16), ((1,), (1,)))
    lane_block = lax.broadcasted_iota(jnp.int32, (mem_dev, BATCHES * SLOTS), 1) // OB
    prior = jnp.zeros((mem_dev, BATCHES * SLOTS), F32)
    for n in range(BATCHES * CAPB):
        prior = jnp.where(lane_block == n, each[n * mem_dev : (n + 1) * mem_dev], prior)
    mean = jnp.sum(prior, 0, keepdims=True) / mem_dev
    mean_high, mean_low = two_parts(mean)
    row = lax.broadcasted_iota(jnp.int32, (ROWS - mem_dev, BATCHES * SLOTS), 0)
    tail = jnp.where(row == 0, mean_high, jnp.where(row == 1, mean_low, 0.0))
    block = jnp.concatenate([prior - mean, tail], 0).astype(BF16)
    for g in range(out_ref.shape[0]):
        out_ref[g] = block


def gather_small_kernel(counts_ref, index_ref, mask_ref, observed_ref, error_ref, between_ref, own_ref, slots_ref):
    columns, _, blocks = mask_ref.shape
    lane_block = lax.broadcasted_iota(jnp.int32, (1, SLOTS), 1) // OB
    wanted = jnp.zeros((1, SLOTS), jnp.int32)
    for b in range(CAPB):
        wanted = jnp.where(lane_block == b, index_ref[1, b], wanted)
    chosen = (lax.broadcasted_iota(jnp.int32, (blocks, SLOTS), 0) == wanted).astype(F32).astype(BF16)
    mask = mask_ref[...].astype(F32).astype(BF16)
    between_ref[...] = dot(mask[:, 0], chosen, ((1,), (0,)))
    cells = own_ref.shape[2]
    block = lax.broadcasted_iota(jnp.int32, (blocks, cells), 1) // BLK + lax.axis_index("mem") * (cells // BLK)
    mine = (lax.broadcasted_iota(jnp.int32, (blocks, cells), 0) == block).astype(F32).astype(BF16)
    for k in range(BATCHES):
        own_ref[k] = dot(mask[:, k], mine, ((1,), (0,)))
        slots_ref[3 * k : 3 * k + 1] = observed_ref[k : k + 1]
        slots_ref[3 * k + 1 : 3 * k + 2] = error_ref[k : k + 1]
        slots_ref[3 * k + 2 : 3 * k + 3] = (lane_block < counts_ref[k, 0]).astype(F32)


def members_of(shared_ref, batch_id):
    groups = shared_ref.shape[0]
    mem_dev = MEMBERS // groups
    lanes = slice(batch_id * SLOTS, (batch_id + 1) * SLOTS)
    parts = []
    for g in range(groups):
        block = shared_ref[g, :, lanes].astype(F32)
        parts.append(block[:mem_dev] + (block[mem_dev : mem_dev + 1] + block[mem_dev + 1 : mem_dev + 2]))
    return jnp.concatenate(parts, 0)


def store_packed(out_ref, prior, slots):
    observed, error_now, live = slots[0:1], slots[1:2], slots[2:3] > 0.5
    mean_obs = jnp.sum(prior, 0, keepdims=True) / MEMBERS
    spread = prior - mean_obs
    variance = jnp.sum(spread * spread, 0, keepdims=True) / (MEMBERS - 1)
    gain = 1.0 / (variance + error_now)
    shrink = gain / (1.0 + jnp.sqrt(error_now * gain))
    scale = jnp.sqrt(shrink / (MEMBERS - 1))
    level = jnp.where(live, gain * (observed - mean_obs) / (scale * (MEMBERS - 1)), 0.0)
    scaled = (spread * jnp.where(live, scale, 0.0)).astype(BF16)
    total = jnp.sum(scaled.astype(F32), 0, keepdims=True)
    level_high, level_low = two_parts(level)
    total_high, total_low = two_parts(total)
    row = lax.broadcasted_iota(jnp.int32, (PACK - MEMBERS, SLOTS), 0)
    tail = jnp.where(
        row == 0,
        level_high,
        jnp.where(row == 1, level_low, jnp.where(row == 2, total_high, jnp.where(row == 3, total_low, 0.0))),
    )
    out_ref[:MEMBERS] = scaled
    out_ref[MEMBERS:] = tail.astype(BF16)


def first_pack_kernel(shared_ref, slots_ref, out_ref):
    store_packed(out_ref, members_of(shared_ref, 0), slots_ref[0:3])


def window(own_ref, around_ref):
    tile = lax.axis_index("space")
    below, below_two = 1 - tile % 2, 1 - tile // 2 % 2
    return [
        (0, own_ref),
        (-1, around_ref.at[below, 0]),
        (-2, around_ref.at[below_two, 1]),
        (1, around_ref.at[1 - below, 0]),
        (2, around_ref.at[1 - below_two, 1]),
    ]


def turned(pack):
    return jnp.transpose(pack[:MEMBERS])


def applied(change):
    return (change[MEMBERS : MEMBERS + 1] + change[MEMBERS + 1 : MEMBERS + 2]) - change[:MEMBERS]


def second_pack_kernel(flags_ref, shared_ref, own_ref, around_ref, slots_ref, out_ref):
    prior = members_of(shared_ref, 1)
    high, low = two_parts(prior - jnp.sum(prior, 0, keepdims=True) / MEMBERS)
    deviation = jnp.concatenate([high, low], 1).astype(BF16)
    change = jnp.zeros((PACK, 2 * SLOTS), F32)
    for offset, pack_ref in window(own_ref, around_ref):
        pack = pack_ref[...]
        covariance = dot(turned(pack), deviation, ((1,), (0,)))
        covariance = covariance[:, :SLOTS] + covariance[:, SLOTS:]
        kept = []
        for c in range(CAPB):
            column = (offset + 2) * CAPB + c
            kept.append(covariance[c * OB : (c + 1) * OB] * flags_ref[column : column + 1])
        high, low = two_parts(jnp.concatenate(kept, 0))
        change = change + dot(pack, jnp.concatenate([high, low], 1).astype(BF16), ((1,), (0,)))
    prior = prior + applied(change[:, :SLOTS] + change[:, SLOTS:])
    store_packed(out_ref, prior, slots_ref[3:6])


def update_kernel(
    batch_id, flags_ref, own_ref, around_ref, state_ref, out_ref, turned_ref, packs_ref, total_ref, kept_ref
):
    tiles = window(own_ref, around_ref)
    for n, (_, pack_ref) in enumerate(tiles):
        span = slice(n * SLOTS, (n + 1) * SLOTS)
        turned_ref[span] = turned(pack_ref[...])
        packs_ref[:, span] = pack_ref[...]
    packs_ref[:, 5 * SLOTS :] = tiles[4][1][...]
    total_ref[...] = dot(turned_ref[...], jnp.ones((MEMBERS, BLK), BF16), ((1,), (0,)))
    cells = state_ref.shape[1]
    step = 2 * BLK
    last = 4 * SLOTS

    def covariances(at):
        buffer = at // step % 2
        values = state_ref[:, at : at + step]
        mean = jnp.sum(values.astype(F32), 0, keepdims=True) / MEMBERS
        covariance = dot(turned_ref[...], values, ((1,), (0,)))
        for n, (offset, _) in enumerate(tiles):
            for c in range(CAPB):
                row = n * SLOTS + c * OB
                column = (offset + 2) * CAPB + c
                flags = flags_ref[batch_id, column : column + 1, at : at + step]
                total = total_ref[row : row + OB]
                total = jnp.concatenate([total, total], 1)
                kept = (covariance[row : row + OB] - total * mean) * flags
                high, low = two_parts(kept)
                kept_ref[buffer, row : row + OB] = high.astype(BF16)
                low_row = row + (SLOTS if n == 4 else 6 * SLOTS)
                kept_ref[buffer, low_row : low_row + OB] = low.astype(BF16)

    def apply(at):
        buffer = at // step % 2
        change = (
            dot(packs_ref[:, :last], kept_ref[buffer, :last], ((1,), (0,)))
            + dot(packs_ref[:, last:], kept_ref[buffer, last : 6 * SLOTS], ((1,), (0,)))
            + dot(packs_ref[:, :last], kept_ref[buffer, 6 * SLOTS :], ((1,), (0,)))
        )
        values = state_ref[:, at : at + step].astype(F32)
        out_ref[:, at : at + step] = (values + applied(change)).astype(BF16)

    covariances(0)
    for at in range(0, cells, step):
        if at + step < cells:
            covariances(at + step)
        apply(at)


PARAMS = pltpu.CompilerParams(vmem_limit_bytes=32 * 1024 * 1024)
VM = pl.BlockSpec(memory_space=pltpu.VMEM)
SM = pl.BlockSpec(memory_space=pltpu.SMEM)


def observe(block_index, gate_operator, prior_state, groups):
    mem_dev = prior_state.shape[0]
    anywhere = pl.BlockSpec(memory_space=pltpu.HBM)
    return pl.pallas_call(
        observe_kernel,
        in_specs=[anywhere, anywhere, anywhere],
        out_specs=VM,
        out_shape=jax.ShapeDtypeStruct((groups, ROWS, BATCHES * SLOTS), BF16),
        scratch_shapes=[
            pltpu.SMEM(block_index.shape, jnp.int32),
            pltpu.VMEM(gate_operator.shape, F32),
            pltpu.VMEM((BATCHES * CAPB, mem_dev, BLK), BF16),
            pltpu.SemaphoreType.DMA(()),
            pltpu.SemaphoreType.DMA(()),
            pltpu.SemaphoreType.DMA((BATCHES * CAPB,)),
        ],
        compiler_params=pltpu.CompilerParams(vmem_limit_bytes=64 * 1024 * 1024 - 65536),
        name="observe",
    )(block_index, gate_operator, prior_state)


def gather_small(counts, index, local_mask, observed, errors, cells):
    columns = local_mask.shape[2]
    return pl.pallas_call(
        gather_small_kernel,
        in_specs=[SM, SM, VM, VM, VM],
        out_specs=[VM, VM, VM],
        out_shape=[
            jax.ShapeDtypeStruct((columns, SLOTS), F32),
            jax.ShapeDtypeStruct((BATCHES, columns, cells), F32),
            jax.ShapeDtypeStruct((3 * BATCHES, SLOTS), F32),
        ],
        compiler_params=PARAMS,
        name="gather_small",
    )(counts, index, local_mask.transpose(2, 0, 1), observed, errors)


def first_pack(shared, slots):
    return pl.pallas_call(
        first_pack_kernel,
        in_specs=[VM, VM],
        out_specs=VM,
        out_shape=jax.ShapeDtypeStruct((PACK, SLOTS), BF16),
        compiler_params=PARAMS,
        name="first_pack",
    )(shared, slots)


def second_pack(flags, shared, own, around, slots):
    return pl.pallas_call(
        second_pack_kernel,
        in_specs=[VM, VM, VM, VM, VM],
        out_specs=VM,
        out_shape=jax.ShapeDtypeStruct((PACK, SLOTS), BF16),
        compiler_params=PARAMS,
        name="second_pack",
    )(flags, shared, own, around, slots)


def update(batch_id, flags, own, around, state):
    return pl.pallas_call(
        lambda *refs: update_kernel(batch_id, *refs),
        in_specs=[VM, VM, VM, VM],
        out_specs=VM,
        out_shape=jax.ShapeDtypeStruct(state.shape, BF16),
        scratch_shapes=[
            pltpu.VMEM((5 * SLOTS, MEMBERS), BF16),
            pltpu.VMEM((PACK, 6 * SLOTS), BF16),
            pltpu.VMEM((5 * SLOTS, BLK), F32),
            pltpu.VMEM((2, 10 * SLOTS, 2 * BLK), BF16),
        ],
        compiler_params=PARAMS,
        name="update",
    )(flags, own, around, state)


def passed_around(pack):
    tiles, groups = lax.axis_size("space"), lax.axis_size("mem")
    received = []
    for offset in (1, 2):
        pairs = []
        for tile in range(tiles):
            for m in range(groups):
                above = (tile // offset + m) % 2 == 0
                partner = tile + offset if above else tile - offset
                if 0 <= partner < tiles:
                    pairs.append((tile * groups + m, partner * groups + m))
        received.append(lax.ppermute(pack, ("space", "mem"), pairs))
    return jnp.stack(received)


def chip_shared(received):
    groups = lax.axis_size("mem")
    chips = [[2 * chip, 2 * chip + 1] for chip in range(groups // 2)]
    return lax.all_gather(received, "mem", axis=0, axis_index_groups=chips)


def per_device(prior_state, block_counts, block_index, gate_operator, observed, obs_error, local_mask):
    groups = lax.axis_size("mem")
    mem_dev, cells = prior_state.shape
    own_block = observe(block_index, gate_operator, prior_state, groups)
    shared = lax.all_to_all(own_block, "mem", split_axis=0, concat_axis=0, tiled=True)
    prior_state, local_mask, own_block = lax.optimization_barrier((prior_state, local_mask, own_block))
    moved = prior_state.reshape(mem_dev, groups, cells // groups).transpose(1, 0, 2)
    between, flags, slots = gather_small(
        block_counts, block_index, local_mask, observed, obs_error, cells // groups
    )
    moved, between, flags, slots = lax.optimization_barrier((moved, between, flags, slots))
    state = lax.all_to_all(moved, "mem", split_axis=0, concat_axis=0, tiled=True)
    state = state.reshape(MEMBERS, cells // groups)
    pack = first_pack(shared, slots)
    around = chip_shared(passed_around(pack))
    next_pack = second_pack(between, shared, pack, around, slots)
    next_pack, state = lax.optimization_barrier((next_pack, state))
    received = passed_around(next_pack)
    state = update(0, flags, pack, around, state)
    received, state = lax.optimization_barrier((received, state))
    next_around = chip_shared(received)
    state = update(1, flags, next_pack, next_around, state)
    parts = lax.all_to_all(
        state.reshape(groups, mem_dev, cells // groups), "mem", split_axis=0, concat_axis=0, tiled=True
    )
    return parts.transpose(1, 0, 2).reshape(mem_dev, cells)


def solution(mesh):
    placed = (
        P("mem", "space"),
        P(None, "space"),
        P(None, "space"),
        P(None, "space", None, None),
        P(None, "space"),
        P(None, "space"),
        P(None, "space", None),
    )
    return jax.shard_map(
        per_device, mesh=mesh, in_specs=placed, out_specs=P("mem", "space"), check_vma=False
    )
```

```python
import jax
import jax.numpy as jnp
from jax import lax
from jax.experimental import pallas as pl
from jax.experimental.pallas import tpu as pltpu
from jax.sharding import PartitionSpec as P

MEMBERS = 256
BLK = 128
OB = 32
CAPB = 4
SB = 96
SLOTS = 128
BATCHES = 2
ROWS = 48
PACK = 272
F32 = jnp.float32
BF16 = jnp.bfloat16


def two_parts(value):
    high = value.astype(BF16).astype(F32)
    return high, value - high


def dot(a, b, dims):
    return lax.dot_general(a, b, (dims, ((), ())), preferred_element_type=F32)


def observe_kernel(index_hbm, gate_hbm, state_hbm, out_ref, index_ref, gate, state, index_sem, gate_sem, state_sem):
    index_copy = pltpu.make_async_copy(index_hbm, index_ref, index_sem)
    gate_copy = pltpu.make_async_copy(gate_hbm, gate, gate_sem)
    state_copy = pltpu.make_async_copy(state_hbm, state, state_sem)
    copies = [index_copy, state_copy, gate_copy]
    for copy in copies:
        copy.start()
    for copy in copies:
        copy.wait()
    mem_dev = state.shape[0]
    high, low = two_parts(gate[...].reshape(BATCHES * CAPB * OB, BLK))
    picks = []
    for k in range(BATCHES):
        for c in range(CAPB):
            start = pl.multiple_of(index_ref[k, c] * BLK, BLK)
            picks.append(state[:, pl.ds(start, BLK)])
    rows = jnp.concatenate(picks, 0)
    each = dot(rows, high.astype(BF16), ((1,), (1,))) + dot(rows, low.astype(BF16), ((1,), (1,)))
    lane_block = lax.broadcasted_iota(jnp.int32, (mem_dev, BATCHES * SLOTS), 1) // OB
    prior = jnp.zeros((mem_dev, BATCHES * SLOTS), F32)
    for n in range(BATCHES * CAPB):
        prior = jnp.where(lane_block == n, each[n * mem_dev : (n + 1) * mem_dev], prior)
    mean = jnp.sum(prior, 0, keepdims=True) / mem_dev
    mean_high, mean_low = two_parts(mean)
    row = lax.broadcasted_iota(jnp.int32, (ROWS - mem_dev, BATCHES * SLOTS), 0)
    tail = jnp.where(row == 0, mean_high, jnp.where(row == 1, mean_low, 0.0))
    block = jnp.concatenate([prior - mean, tail], 0).astype(BF16)
    for g in range(out_ref.shape[0]):
        out_ref[g] = block


def gather_small_kernel(counts_ref, index_ref, mask_ref, observed_ref, error_ref, between_ref, own_ref, slots_ref):
    columns, _, blocks = mask_ref.shape
    lane_block = lax.broadcasted_iota(jnp.int32, (1, SLOTS), 1) // OB
    wanted = jnp.zeros((1, SLOTS), jnp.int32)
    for b in range(CAPB):
        wanted = jnp.where(lane_block == b, index_ref[1, b], wanted)
    chosen = (lax.broadcasted_iota(jnp.int32, (blocks, SLOTS), 0) == wanted).astype(F32).astype(BF16)
    mask = mask_ref[...].astype(F32).astype(BF16)
    between_ref[...] = dot(mask[:, 0], chosen, ((1,), (0,)))
    cells = own_ref.shape[2]
    block = lax.broadcasted_iota(jnp.int32, (blocks, cells), 1) // BLK + lax.axis_index("mem") * (cells // BLK)
    mine = (lax.broadcasted_iota(jnp.int32, (blocks, cells), 0) == block).astype(F32).astype(BF16)
    for k in range(BATCHES):
        own_ref[k] = dot(mask[:, k], mine, ((1,), (0,)))
        slots_ref[3 * k : 3 * k + 1] = observed_ref[k : k + 1]
        slots_ref[3 * k + 1 : 3 * k + 2] = error_ref[k : k + 1]
        slots_ref[3 * k + 2 : 3 * k + 3] = (lane_block < counts_ref[k, 0]).astype(F32)


def members_of(shared_ref, batch_id):
    groups = shared_ref.shape[0]
    mem_dev = MEMBERS // groups
    lanes = slice(batch_id * SLOTS, (batch_id + 1) * SLOTS)
    parts = []
    for g in range(groups):
        block = shared_ref[g, :, lanes].astype(F32)
        parts.append(block[:mem_dev] + (block[mem_dev : mem_dev + 1] + block[mem_dev + 1 : mem_dev + 2]))
    return jnp.concatenate(parts, 0)


def store_packed(out_ref, prior, slots):
    observed, error_now, live = slots[0:1], slots[1:2], slots[2:3] > 0.5
    mean_obs = jnp.sum(prior, 0, keepdims=True) / MEMBERS
    spread = prior - mean_obs
    variance = jnp.sum(spread * spread, 0, keepdims=True) / (MEMBERS - 1)
    gain = 1.0 / (variance + error_now)
    shrink = gain / (1.0 + jnp.sqrt(error_now * gain))
    scale = jnp.sqrt(shrink / (MEMBERS - 1))
    level = jnp.where(live, gain * (observed - mean_obs) / (scale * (MEMBERS - 1)), 0.0)
    scaled = (spread * jnp.where(live, scale, 0.0)).astype(BF16)
    total = jnp.sum(scaled.astype(F32), 0, keepdims=True)
    level_high, level_low = two_parts(level)
    total_high, total_low = two_parts(total)
    row = lax.broadcasted_iota(jnp.int32, (PACK - MEMBERS, SLOTS), 0)
    tail = jnp.where(
        row == 0,
        level_high,
        jnp.where(row == 1, level_low, jnp.where(row == 2, total_high, jnp.where(row == 3, total_low, 0.0))),
    )
    out_ref[:MEMBERS] = scaled
    out_ref[MEMBERS:] = tail.astype(BF16)


def first_pack_kernel(shared_ref, slots_ref, out_ref):
    store_packed(out_ref, members_of(shared_ref, 0), slots_ref[0:3])


def window(own_ref, around_ref):
    tile = lax.axis_index("space")
    odd, upper = tile % 2, tile // 2 % 2
    return [
        (0, own_ref),
        (-1, around_ref.at[3 - 3 * odd]),
        (-2, around_ref.at[1 + upper]),
        (1, around_ref.at[3 * odd]),
        (2, around_ref.at[2 - upper]),
    ]


def turned(pack):
    return jnp.transpose(pack[:MEMBERS])


def applied(change):
    return (change[MEMBERS : MEMBERS + 1] + change[MEMBERS + 1 : MEMBERS + 2]) - change[:MEMBERS]


def second_pack_kernel(flags_ref, shared_ref, own_ref, around_ref, slots_ref, out_ref):
    prior = members_of(shared_ref, 1)
    high, low = two_parts(prior - jnp.sum(prior, 0, keepdims=True) / MEMBERS)
    deviation = jnp.concatenate([high, low], 1).astype(BF16)
    change = jnp.zeros((PACK, 2 * SLOTS), F32)
    for offset, pack_ref in window(own_ref, around_ref):
        pack = pack_ref[...]
        covariance = dot(turned(pack), deviation, ((1,), (0,)))
        covariance = covariance[:, :SLOTS] + covariance[:, SLOTS:]
        kept = []
        for c in range(CAPB):
            column = (offset + 2) * CAPB + c
            kept.append(covariance[c * OB : (c + 1) * OB] * flags_ref[column : column + 1])
        high, low = two_parts(jnp.concatenate(kept, 0))
        change = change + dot(pack, jnp.concatenate([high, low], 1).astype(BF16), ((1,), (0,)))
    prior = prior + applied(change[:, :SLOTS] + change[:, SLOTS:])
    store_packed(out_ref, prior, slots_ref[3:6])


def update_kernel(
    batch_id, flags_ref, own_ref, around_ref, state_ref, out_ref, turned_ref, packs_ref, total_ref, kept_ref
):
    tiles = window(own_ref, around_ref)
    for n, (_, pack_ref) in enumerate(tiles):
        span = slice(n * SLOTS, (n + 1) * SLOTS)
        turned_ref[span] = turned(pack_ref[...])
        packs_ref[:, span] = pack_ref[...]
    packs_ref[:, 5 * SLOTS :] = tiles[4][1][...]
    total_ref[...] = dot(turned_ref[...], jnp.ones((MEMBERS, BLK), BF16), ((1,), (0,)))
    cells = state_ref.shape[1]
    step = 2 * BLK
    last = 4 * SLOTS

    def covariances(at):
        buffer = at // step % 2
        values = state_ref[:, at : at + step]
        mean = jnp.sum(values.astype(F32), 0, keepdims=True) / MEMBERS
        covariance = dot(turned_ref[...], values, ((1,), (0,)))
        for n, (offset, _) in enumerate(tiles):
            for c in range(CAPB):
                row = n * SLOTS + c * OB
                column = (offset + 2) * CAPB + c
                flags = flags_ref[batch_id, column : column + 1, at : at + step]
                total = total_ref[row : row + OB]
                total = jnp.concatenate([total, total], 1)
                kept = (covariance[row : row + OB] - total * mean) * flags
                high, low = two_parts(kept)
                kept_ref[buffer, row : row + OB] = high.astype(BF16)
                low_row = row + (SLOTS if n == 4 else 6 * SLOTS)
                kept_ref[buffer, low_row : low_row + OB] = low.astype(BF16)

    def apply(at):
        buffer = at // step % 2
        change = (
            dot(packs_ref[:, :last], kept_ref[buffer, :last], ((1,), (0,)))
            + dot(packs_ref[:, last:], kept_ref[buffer, last : 6 * SLOTS], ((1,), (0,)))
            + dot(packs_ref[:, :last], kept_ref[buffer, 6 * SLOTS :], ((1,), (0,)))
        )
        values = state_ref[:, at : at + step].astype(F32)
        out_ref[:, at : at + step] = (values + applied(change)).astype(BF16)

    covariances(0)
    for at in range(0, cells, step):
        if at + step < cells:
            covariances(at + step)
        apply(at)


PARAMS = pltpu.CompilerParams(vmem_limit_bytes=32 * 1024 * 1024)
VM = pl.BlockSpec(memory_space=pltpu.VMEM)
SM = pl.BlockSpec(memory_space=pltpu.SMEM)


def observe(block_index, gate_operator, prior_state, groups):
    mem_dev = prior_state.shape[0]
    anywhere = pl.BlockSpec(memory_space=pltpu.HBM)
    return pl.pallas_call(
        observe_kernel,
        in_specs=[anywhere, anywhere, anywhere],
        out_specs=VM,
        out_shape=jax.ShapeDtypeStruct((groups, ROWS, BATCHES * SLOTS), BF16),
        scratch_shapes=[
            pltpu.SMEM(block_index.shape, jnp.int32),
            pltpu.VMEM(gate_operator.shape, F32),
            pltpu.VMEM(prior_state.shape, BF16),
            pltpu.SemaphoreType.DMA(()),
            pltpu.SemaphoreType.DMA(()),
            pltpu.SemaphoreType.DMA(()),
        ],
        compiler_params=pltpu.CompilerParams(vmem_limit_bytes=64 * 1024 * 1024 - 65536),
        name="observe",
    )(block_index, gate_operator, prior_state)


def gather_small(counts, index, local_mask, observed, errors, cells):
    columns = local_mask.shape[2]
    return pl.pallas_call(
        gather_small_kernel,
        in_specs=[SM, SM, VM, VM, VM],
        out_specs=[VM, VM, VM],
        out_shape=[
            jax.ShapeDtypeStruct((columns, SLOTS), F32),
            jax.ShapeDtypeStruct((BATCHES, columns, cells), F32),
            jax.ShapeDtypeStruct((3 * BATCHES, SLOTS), F32),
        ],
        compiler_params=PARAMS,
        name="gather_small",
    )(counts, index, local_mask.transpose(2, 0, 1), observed, errors)


def first_pack(shared, slots):
    return pl.pallas_call(
        first_pack_kernel,
        in_specs=[VM, VM],
        out_specs=VM,
        out_shape=jax.ShapeDtypeStruct((PACK, SLOTS), BF16),
        compiler_params=PARAMS,
        name="first_pack",
    )(shared, slots)


def second_pack(flags, shared, own, around, slots):
    return pl.pallas_call(
        second_pack_kernel,
        in_specs=[VM, VM, VM, VM, VM],
        out_specs=VM,
        out_shape=jax.ShapeDtypeStruct((PACK, SLOTS), BF16),
        compiler_params=PARAMS,
        name="second_pack",
    )(flags, shared, own, around, slots)


def update(batch_id, flags, own, around, state):
    return pl.pallas_call(
        lambda *refs: update_kernel(batch_id, *refs),
        in_specs=[VM, VM, VM, VM],
        out_specs=VM,
        out_shape=jax.ShapeDtypeStruct(state.shape, BF16),
        scratch_shapes=[
            pltpu.VMEM((5 * SLOTS, MEMBERS), BF16),
            pltpu.VMEM((PACK, 6 * SLOTS), BF16),
            pltpu.VMEM((5 * SLOTS, BLK), F32),
            pltpu.VMEM((2, 10 * SLOTS, 2 * BLK), BF16),
        ],
        compiler_params=PARAMS,
        name="update",
    )(flags, own, around, state)


def swapped(pack, across):
    tiles, groups = lax.axis_size("space"), lax.axis_size("mem")
    pairs = []
    for tile in range(tiles):
        for m in range(groups):
            offset = 1 if m % 2 == across else 2
            above = tile // offset % 2 == across
            partner = tile + offset if above else tile - offset
            if 0 <= partner < tiles:
                pairs.append((tile * groups + m, partner * groups + m))
    return lax.ppermute(pack, ("space", "mem"), pairs)


def passed_around(pack):
    return jnp.stack([swapped(pack, 0), swapped(pack, 1)])


def chip_shared(received):
    groups = lax.axis_size("mem")
    chips = [[2 * chip, 2 * chip + 1] for chip in range(groups // 2)]
    return lax.all_gather(received, "mem", axis=0, axis_index_groups=chips, tiled=True)


def per_device(prior_state, block_counts, block_index, gate_operator, observed, obs_error, local_mask):
    groups = lax.axis_size("mem")
    mem_dev, cells = prior_state.shape
    own_block = observe(block_index, gate_operator, prior_state, groups)
    shared = lax.all_to_all(own_block, "mem", split_axis=0, concat_axis=0, tiled=True)
    prior_state, local_mask, own_block = lax.optimization_barrier((prior_state, local_mask, own_block))
    moved = prior_state.reshape(mem_dev, groups, cells // groups).transpose(1, 0, 2)
    between, flags, slots = gather_small(
        block_counts, block_index, local_mask, observed, obs_error, cells // groups
    )
    moved, between, flags, slots = lax.optimization_barrier((moved, between, flags, slots))
    state = lax.all_to_all(moved, "mem", split_axis=0, concat_axis=0, tiled=True)
    state = state.reshape(MEMBERS, cells // groups)
    pack = first_pack(shared, slots)
    around = chip_shared(passed_around(pack))
    next_pack = second_pack(between, shared, pack, around, slots)
    next_pack, state = lax.optimization_barrier((next_pack, state))
    received = passed_around(next_pack)
    state = update(0, flags, pack, around, state)
    received, state = lax.optimization_barrier((received, state))
    next_around = chip_shared(received)
    state = update(1, flags, next_pack, next_around, state)
    parts = lax.all_to_all(
        state.reshape(groups, mem_dev, cells // groups), "mem", split_axis=0, concat_axis=0, tiled=True
    )
    return parts.transpose(1, 0, 2).reshape(mem_dev, cells)


def solution(mesh):
    placed = (
        P("mem", "space"),
        P(None, "space"),
        P(None, "space"),
        P(None, "space", None, None),
        P(None, "space"),
        P(None, "space"),
        P(None, "space", None),
    )
    return jax.shard_map(
        per_device, mesh=mesh, in_specs=placed, out_specs=P("mem", "space"), check_vma=False
    )
```

```python
import jax
import jax.numpy as jnp
from jax import lax
from jax.experimental import pallas as pl
from jax.experimental.pallas import tpu as pltpu
from jax.sharding import PartitionSpec as P

MEMBERS = 256
ROW = 16
BLK = 128
OB = 32
CAPB = 4
SLOTS = 128
BATCHES = 2
PACK = 272
F32 = jnp.float32
BF16 = jnp.bfloat16


def two_parts(value):
    high = value.astype(BF16).astype(F32)
    return high, value - high


def dot(a, b, dims):
    return lax.dot_general(a, b, (dims, ((), ())), preferred_element_type=F32)


def observe_kernel(index_hbm, gate_hbm, state_hbm, out_ref, index_ref, gate, state, index_sem, gate_sem, state_sem):
    index_copy = pltpu.make_async_copy(index_hbm, index_ref, index_sem)
    gate_copy = pltpu.make_async_copy(gate_hbm, gate, gate_sem)
    state_copy = pltpu.make_async_copy(state_hbm, state, state_sem)
    copies = [index_copy, state_copy, gate_copy]
    for copy in copies:
        copy.start()
    for copy in copies:
        copy.wait()
    mem_dev = state.shape[0]
    high, low = two_parts(gate[...].reshape(BATCHES * CAPB * OB, BLK))
    picks = []
    for k in range(BATCHES):
        for c in range(CAPB):
            start = pl.multiple_of(index_ref[k, c] * BLK, BLK)
            picks.append(state[:, pl.ds(start, BLK)])
    rows = jnp.concatenate(picks, 0)
    each = dot(rows, high.astype(BF16), ((1,), (1,))) + dot(rows, low.astype(BF16), ((1,), (1,)))
    lane_block = lax.broadcasted_iota(jnp.int32, (mem_dev, BATCHES * SLOTS), 1) // OB
    prior = jnp.zeros((mem_dev, BATCHES * SLOTS), F32)
    for n in range(BATCHES * CAPB):
        prior = jnp.where(lane_block == n, each[n * mem_dev : (n + 1) * mem_dev], prior)
    for g in range(out_ref.shape[0]):
        out_ref[g] = prior


def gather_small_kernel(counts_ref, index_ref, mask_ref, observed_ref, error_ref, between_ref, own_ref, slots_ref):
    columns, _, blocks = mask_ref.shape
    lane_block = lax.broadcasted_iota(jnp.int32, (1, SLOTS), 1) // OB
    wanted = jnp.zeros((1, SLOTS), jnp.int32)
    for b in range(CAPB):
        wanted = jnp.where(lane_block == b, index_ref[1, b], wanted)
    chosen = (lax.broadcasted_iota(jnp.int32, (blocks, SLOTS), 0) == wanted).astype(F32).astype(BF16)
    mask = mask_ref[...].astype(F32).astype(BF16)
    between_ref[...] = dot(mask[:, 0], chosen, ((1,), (0,)))
    cells = own_ref.shape[2]
    block = lax.broadcasted_iota(jnp.int32, (blocks, cells), 1) // BLK + lax.axis_index("mem") * (cells // BLK)
    mine = (lax.broadcasted_iota(jnp.int32, (blocks, cells), 0) == block).astype(F32).astype(BF16)
    for k in range(BATCHES):
        own_ref[k] = dot(mask[:, k], mine, ((1,), (0,)))
        slots_ref[3 * k : 3 * k + 1] = observed_ref[k : k + 1]
        slots_ref[3 * k + 1 : 3 * k + 2] = error_ref[k : k + 1]
        slots_ref[3 * k + 2 : 3 * k + 3] = (lane_block < counts_ref[k, 0]).astype(F32)


def members_of(shared_ref, batch_id):
    groups, mem_dev, _ = shared_ref.shape
    lanes = slice(batch_id * SLOTS, (batch_id + 1) * SLOTS)
    return shared_ref[:, :, lanes].reshape(groups * mem_dev, SLOTS)


def store_packed(out_ref, prior, slots):
    observed, error_now, live = slots[0:1], slots[1:2], slots[2:3] > 0.5
    mean_obs = jnp.sum(prior, 0, keepdims=True) / MEMBERS
    spread = prior - mean_obs
    variance = jnp.sum(spread * spread, 0, keepdims=True) / (MEMBERS - 1)
    gain = 1.0 / (variance + error_now)
    shrink = gain / (1.0 + jnp.sqrt(error_now * gain))
    scale = jnp.sqrt(shrink / (MEMBERS - 1))
    level = jnp.where(live, gain * (observed - mean_obs) / (scale * (MEMBERS - 1)), 0.0)
    scaled = (spread * jnp.where(live, scale, 0.0)).astype(BF16)
    total = jnp.sum(scaled.astype(F32), 0, keepdims=True)
    level_high, level_low = two_parts(level)
    total_high, total_low = two_parts(total)
    row = lax.broadcasted_iota(jnp.int32, (PACK - MEMBERS, SLOTS), 0)
    tail = jnp.where(
        row == 0,
        level_high,
        jnp.where(row == 1, level_low, jnp.where(row == 2, total_high, jnp.where(row == 3, total_low, 0.0))),
    )
    out_ref[:MEMBERS] = scaled
    out_ref[MEMBERS:] = tail.astype(BF16)


def first_pack_kernel(shared_ref, slots_ref, out_ref):
    store_packed(out_ref, members_of(shared_ref, 0), slots_ref[0:3])


def window(own_ref, around_ref):
    tile = lax.axis_index("space")
    odd, upper = tile % 2, tile // 2 % 2
    return [
        (0, own_ref),
        (-1, around_ref.at[3 - 3 * odd]),
        (-2, around_ref.at[1 + upper]),
        (1, around_ref.at[3 * odd]),
        (2, around_ref.at[2 - upper]),
    ]


def turned(pack):
    return jnp.transpose(pack[:MEMBERS])


def applied(change):
    return (change[MEMBERS : MEMBERS + 1] + change[MEMBERS + 1 : MEMBERS + 2]) - change[:MEMBERS]


def second_pack_kernel(flags_ref, shared_ref, own_ref, around_ref, slots_ref, out_ref):
    prior = members_of(shared_ref, 1)
    high, low = two_parts(prior - jnp.sum(prior, 0, keepdims=True) / MEMBERS)
    deviation = jnp.concatenate([high, low], 1).astype(BF16)
    change = jnp.zeros((PACK, 2 * SLOTS), F32)
    for offset, pack_ref in window(own_ref, around_ref):
        pack = pack_ref[...]
        covariance = dot(turned(pack), deviation, ((1,), (0,)))
        covariance = covariance[:, :SLOTS] + covariance[:, SLOTS:]
        kept = []
        for c in range(CAPB):
            column = (offset + 2) * CAPB + c
            kept.append(covariance[c * OB : (c + 1) * OB] * flags_ref[column : column + 1])
        high, low = two_parts(jnp.concatenate(kept, 0))
        change = change + dot(pack, jnp.concatenate([high, low], 1).astype(BF16), ((1,), (0,)))
    prior = prior + applied(change[:, :SLOTS] + change[:, SLOTS:])
    store_packed(out_ref, prior, slots_ref[3:6])


def update_kernel(
    batch_id, flags_ref, own_ref, around_ref, state_ref, out_ref, turned_ref, packs_ref, total_ref, kept_ref
):
    tiles = window(own_ref, around_ref)
    for n, (_, pack_ref) in enumerate(tiles):
        span = slice(n * SLOTS, (n + 1) * SLOTS)
        turned_ref[span] = turned(pack_ref[...])
        packs_ref[:, span] = pack_ref[...]
    packs_ref[:, 5 * SLOTS :] = tiles[4][1][...]
    total_ref[...] = dot(turned_ref[...], jnp.ones((MEMBERS, BLK), BF16), ((1,), (0,)))
    cells = state_ref.shape[1]
    step = 2 * BLK
    last = 4 * SLOTS

    def covariances(at):
        buffer = at // step % 2
        values = state_ref[:, at : at + step]
        mean = jnp.sum(values.astype(F32), 0, keepdims=True) / MEMBERS
        covariance = dot(turned_ref[...], values, ((1,), (0,)))
        for n, (offset, _) in enumerate(tiles):
            for c in range(CAPB):
                row = n * SLOTS + c * OB
                column = (offset + 2) * CAPB + c
                flags = flags_ref[batch_id, column : column + 1, at : at + step]
                total = total_ref[row : row + OB]
                total = jnp.concatenate([total, total], 1)
                kept = (covariance[row : row + OB] - total * mean) * flags
                high, low = two_parts(kept)
                kept_ref[buffer, row : row + OB] = high.astype(BF16)
                low_row = row + (SLOTS if n == 4 else 6 * SLOTS)
                kept_ref[buffer, low_row : low_row + OB] = low.astype(BF16)

    def apply(at):
        buffer = at // step % 2
        change = (
            dot(packs_ref[:, :last], kept_ref[buffer, :last], ((1,), (0,)))
            + dot(packs_ref[:, last:], kept_ref[buffer, last : 6 * SLOTS], ((1,), (0,)))
            + dot(packs_ref[:, :last], kept_ref[buffer, 6 * SLOTS :], ((1,), (0,)))
        )
        values = state_ref[:, at : at + step].astype(F32)
        out_ref[:, at : at + step] = (values + applied(change)).astype(BF16)

    covariances(0)
    for at in range(0, cells, step):
        if at + step < cells:
            covariances(at + step)
        apply(at)


PARAMS = pltpu.CompilerParams(vmem_limit_bytes=32 * 1024 * 1024)
VM = pl.BlockSpec(memory_space=pltpu.VMEM)
SM = pl.BlockSpec(memory_space=pltpu.SMEM)


def observe(block_index, gate_operator, prior_state, groups):
    mem_dev = prior_state.shape[0]
    anywhere = pl.BlockSpec(memory_space=pltpu.HBM)
    return pl.pallas_call(
        observe_kernel,
        in_specs=[anywhere, anywhere, anywhere],
        out_specs=VM,
        out_shape=jax.ShapeDtypeStruct((groups, mem_dev, BATCHES * SLOTS), F32),
        scratch_shapes=[
            pltpu.SMEM(block_index.shape, jnp.int32),
            pltpu.VMEM(gate_operator.shape, F32),
            pltpu.VMEM(prior_state.shape, BF16),
            pltpu.SemaphoreType.DMA(()),
            pltpu.SemaphoreType.DMA(()),
            pltpu.SemaphoreType.DMA(()),
        ],
        compiler_params=pltpu.CompilerParams(vmem_limit_bytes=64 * 1024 * 1024 - 65536),
        name="observe",
    )(block_index, gate_operator, prior_state)


def gather_small(counts, index, local_mask, observed, errors, cells):
    columns = local_mask.shape[2]
    return pl.pallas_call(
        gather_small_kernel,
        in_specs=[SM, SM, VM, VM, VM],
        out_specs=[VM, VM, VM],
        out_shape=[
            jax.ShapeDtypeStruct((columns, SLOTS), F32),
            jax.ShapeDtypeStruct((BATCHES, columns, cells), F32),
            jax.ShapeDtypeStruct((3 * BATCHES, SLOTS), F32),
        ],
        compiler_params=PARAMS,
        name="gather_small",
    )(counts, index, local_mask.transpose(2, 0, 1), observed, errors)


def first_pack(shared, slots):
    return pl.pallas_call(
        first_pack_kernel,
        in_specs=[VM, VM],
        out_specs=VM,
        out_shape=jax.ShapeDtypeStruct((PACK, SLOTS), BF16),
        compiler_params=PARAMS,
        name="first_pack",
    )(shared, slots)


def second_pack(flags, shared, own, around, slots):
    return pl.pallas_call(
        second_pack_kernel,
        in_specs=[VM, VM, VM, VM, VM],
        out_specs=VM,
        out_shape=jax.ShapeDtypeStruct((PACK, SLOTS), BF16),
        compiler_params=PARAMS,
        name="second_pack",
    )(flags, shared, own, around, slots)


def update(batch_id, flags, own, around, state):
    return pl.pallas_call(
        lambda *refs: update_kernel(batch_id, *refs),
        in_specs=[VM, VM, VM, VM],
        out_specs=VM,
        out_shape=jax.ShapeDtypeStruct(state.shape, BF16),
        scratch_shapes=[
            pltpu.VMEM((5 * SLOTS, MEMBERS), BF16),
            pltpu.VMEM((PACK, 6 * SLOTS), BF16),
            pltpu.VMEM((5 * SLOTS, BLK), F32),
            pltpu.VMEM((2, 10 * SLOTS, 2 * BLK), BF16),
        ],
        compiler_params=PARAMS,
        name="update",
    )(flags, own, around, state)


def partner_of(tile, m, across):
    offset = 1 if m % 2 == across else 2
    return tile + offset if tile // offset % 2 == across else tile - offset


def swapped(pack, across, wanted):
    tiles, groups = lax.axis_size("space"), lax.axis_size("mem")
    pairs = []
    for tile in range(tiles):
        for m in range(groups):
            partner = partner_of(tile, m, across)
            if 0 <= partner < tiles and wanted(tile):
                pairs.append((tile * groups + m, partner * groups + m))
    return lax.ppermute(pack, ("space", "mem"), pairs)


def passed_around(pack):
    starts = swapped(pack, 0, lambda tile: tile % ROW < ROW // 2)
    across = swapped(pack, 1, lambda tile: True)
    ends = swapped(pack, 0, lambda tile: tile % ROW >= ROW // 2)
    first = lax.optimization_barrier(jnp.stack([across, starts]))
    return jnp.stack([first[1] + ends, first[0]])


def chip_shared(received):
    groups = lax.axis_size("mem")
    chips = [[2 * chip, 2 * chip + 1] for chip in range(groups // 2)]
    return lax.all_gather(received, "mem", axis=0, axis_index_groups=chips, tiled=True)


def per_device(prior_state, block_counts, block_index, gate_operator, observed, obs_error, local_mask):
    groups = lax.axis_size("mem")
    mem_dev, cells = prior_state.shape
    own_block = observe(block_index, gate_operator, prior_state, groups)
    shared = lax.all_to_all(own_block, "mem", split_axis=0, concat_axis=0, tiled=True)
    prior_state, local_mask, own_block = lax.optimization_barrier((prior_state, local_mask, own_block))
    moved = prior_state.reshape(mem_dev, groups, cells // groups).transpose(1, 0, 2)
    between, flags, slots = gather_small(
        block_counts, block_index, local_mask, observed, obs_error, cells // groups
    )
    moved, between, flags, slots = lax.optimization_barrier((moved, between, flags, slots))
    state = lax.all_to_all(moved, "mem", split_axis=0, concat_axis=0, tiled=True)
    state = state.reshape(MEMBERS, cells // groups)
    pack = first_pack(shared, slots)
    around = chip_shared(passed_around(pack))
    next_pack = second_pack(between, shared, pack, around, slots)
    next_pack, state = lax.optimization_barrier((next_pack, state))
    received = passed_around(next_pack)
    state = update(0, flags, pack, around, state)
    received, state = lax.optimization_barrier((received, state))
    next_around = chip_shared(received)
    state = update(1, flags, next_pack, next_around, state)
    parts = lax.all_to_all(
        state.reshape(groups, mem_dev, cells // groups), "mem", split_axis=0, concat_axis=0, tiled=True
    )
    return parts.transpose(1, 0, 2).reshape(mem_dev, cells)


def solution(mesh):
    placed = (
        P("mem", "space"),
        P(None, "space"),
        P(None, "space"),
        P(None, "space", None, None),
        P(None, "space"),
        P(None, "space"),
        P(None, "space", None),
    )
    return jax.shard_map(
        per_device, mesh=mesh, in_specs=placed, out_specs=P("mem", "space"), check_vma=False
    )
```

```python
import jax
import jax.numpy as jnp
from jax import lax
from jax.experimental import pallas as pl
from jax.experimental.pallas import tpu as pltpu
from jax.sharding import PartitionSpec as P

MEMBERS = 256
ROW = 16
BLK = 128
OB = 32
CAPB = 4
SLOTS = 128
BATCHES = 2
PACK = 272
F32 = jnp.float32
BF16 = jnp.bfloat16


def two_parts(value):
    high = value.astype(BF16).astype(F32)
    return high, value - high


def dot(a, b, dims):
    return lax.dot_general(a, b, (dims, ((), ())), preferred_element_type=F32)


def observe_kernel(index_hbm, gate_hbm, state_hbm, out_ref, index_ref, gate, state, index_sem, gate_sem, state_sem):
    index_copy = pltpu.make_async_copy(index_hbm, index_ref, index_sem)
    gate_copy = pltpu.make_async_copy(gate_hbm, gate, gate_sem)
    state_copy = pltpu.make_async_copy(state_hbm, state, state_sem)
    copies = [index_copy, state_copy, gate_copy]
    for copy in copies:
        copy.start()
    for copy in copies:
        copy.wait()
    mem_dev = state.shape[0]
    high, low = two_parts(gate[...].reshape(BATCHES * CAPB * OB, BLK))
    picks = []
    for k in range(BATCHES):
        for c in range(CAPB):
            start = pl.multiple_of(index_ref[k, c] * BLK, BLK)
            picks.append(state[:, pl.ds(start, BLK)])
    rows = jnp.concatenate(picks, 0)
    each = dot(rows, high.astype(BF16), ((1,), (1,))) + dot(rows, low.astype(BF16), ((1,), (1,)))
    lane_block = lax.broadcasted_iota(jnp.int32, (mem_dev, BATCHES * SLOTS), 1) // OB
    prior = jnp.zeros((mem_dev, BATCHES * SLOTS), F32)
    for n in range(BATCHES * CAPB):
        prior = jnp.where(lane_block == n, each[n * mem_dev : (n + 1) * mem_dev], prior)
    for g in range(out_ref.shape[0]):
        out_ref[g] = prior


def gather_small_kernel(counts_ref, index_ref, mask_ref, observed_ref, error_ref, between_ref, own_ref, slots_ref):
    columns, _, blocks = mask_ref.shape
    lane_block = lax.broadcasted_iota(jnp.int32, (1, SLOTS), 1) // OB
    wanted = jnp.zeros((1, SLOTS), jnp.int32)
    for b in range(CAPB):
        wanted = jnp.where(lane_block == b, index_ref[1, b], wanted)
    chosen = (lax.broadcasted_iota(jnp.int32, (blocks, SLOTS), 0) == wanted).astype(F32).astype(BF16)
    mask = mask_ref[...].astype(F32).astype(BF16)
    between_ref[...] = dot(mask[:, 0], chosen, ((1,), (0,)))
    cells = own_ref.shape[2]
    block = lax.broadcasted_iota(jnp.int32, (blocks, cells), 1) // BLK + lax.axis_index("mem") * (cells // BLK)
    mine = (lax.broadcasted_iota(jnp.int32, (blocks, cells), 0) == block).astype(F32).astype(BF16)
    for k in range(BATCHES):
        own_ref[k] = dot(mask[:, k], mine, ((1,), (0,)))
        slots_ref[3 * k : 3 * k + 1] = observed_ref[k : k + 1]
        slots_ref[3 * k + 1 : 3 * k + 2] = error_ref[k : k + 1]
        slots_ref[3 * k + 2 : 3 * k + 3] = (lane_block < counts_ref[k, 0]).astype(F32)


def members_of(shared_ref, batch_id):
    groups, mem_dev, _ = shared_ref.shape
    lanes = slice(batch_id * SLOTS, (batch_id + 1) * SLOTS)
    return shared_ref[:, :, lanes].reshape(groups * mem_dev, SLOTS)


def store_packed(out_ref, prior, slots):
    observed, error_now, live = slots[0:1], slots[1:2], slots[2:3] > 0.5
    mean_obs = jnp.sum(prior, 0, keepdims=True) / MEMBERS
    spread = prior - mean_obs
    variance = jnp.sum(spread * spread, 0, keepdims=True) / (MEMBERS - 1)
    gain = 1.0 / (variance + error_now)
    shrink = gain / (1.0 + jnp.sqrt(error_now * gain))
    scale = jnp.sqrt(shrink / (MEMBERS - 1))
    level = jnp.where(live, gain * (observed - mean_obs) / (scale * (MEMBERS - 1)), 0.0)
    scaled = (spread * jnp.where(live, scale, 0.0)).astype(BF16)
    total = jnp.sum(scaled.astype(F32), 0, keepdims=True)
    level_high, level_low = two_parts(level)
    total_high, total_low = two_parts(total)
    row = lax.broadcasted_iota(jnp.int32, (PACK - MEMBERS, SLOTS), 0)
    tail = jnp.where(
        row == 0,
        level_high,
        jnp.where(row == 1, level_low, jnp.where(row == 2, total_high, jnp.where(row == 3, total_low, 0.0))),
    )
    out_ref[:MEMBERS] = scaled
    out_ref[MEMBERS:] = tail.astype(BF16)


def first_pack_kernel(shared_ref, slots_ref, out_ref):
    store_packed(out_ref, members_of(shared_ref, 0), slots_ref[0:3])


def window(own_ref, around_ref):
    tile = lax.axis_index("space")
    odd, upper = tile % 2, tile // 2 % 2
    return [
        (0, own_ref),
        (-1, around_ref.at[3 - 3 * odd]),
        (-2, around_ref.at[1 + upper]),
        (1, around_ref.at[3 * odd]),
        (2, around_ref.at[2 - upper]),
    ]


def turned(pack):
    return jnp.transpose(pack[:MEMBERS])


def applied(change):
    return (change[MEMBERS : MEMBERS + 1] + change[MEMBERS + 1 : MEMBERS + 2]) - change[:MEMBERS]


def second_pack_kernel(flags_ref, shared_ref, own_ref, around_ref, slots_ref, out_ref):
    prior = members_of(shared_ref, 1)
    high, low = two_parts(prior - jnp.sum(prior, 0, keepdims=True) / MEMBERS)
    deviation = jnp.concatenate([high, low], 1).astype(BF16)
    tiles = [(offset, pack_ref[...]) for offset, pack_ref in window(own_ref, around_ref)]
    covariance = dot(jnp.concatenate([turned(pack) for _, pack in tiles], 0), deviation, ((1,), (0,)))
    covariance = covariance[:, :SLOTS] + covariance[:, SLOTS:]
    kept = []
    for n, (offset, _) in enumerate(tiles):
        for c in range(CAPB):
            column = (offset + 2) * CAPB + c
            row = n * SLOTS + c * OB
            kept.append(covariance[row : row + OB] * flags_ref[column : column + 1])
    high, low = two_parts(jnp.concatenate(kept, 0))
    parts = jnp.concatenate([high, low], 1).astype(BF16)
    change = dot(jnp.concatenate([pack for _, pack in tiles], 1), parts, ((1,), (0,)))
    prior = prior + applied(change[:, :SLOTS] + change[:, SLOTS:])
    store_packed(out_ref, prior, slots_ref[3:6])


def update_kernel(
    batch_id, flags_ref, own_ref, around_ref, state_ref, out_ref, turned_ref, packs_ref, total_ref, kept_ref
):
    tiles = window(own_ref, around_ref)
    for n, (_, pack_ref) in enumerate(tiles):
        span = slice(n * SLOTS, (n + 1) * SLOTS)
        turned_ref[span] = turned(pack_ref[...])
        packs_ref[:, span] = pack_ref[...]
    packs_ref[:, 5 * SLOTS :] = tiles[4][1][...]
    total_ref[...] = dot(turned_ref[...], jnp.ones((MEMBERS, BLK), BF16), ((1,), (0,)))
    cells = state_ref.shape[1]
    step = 2 * BLK
    last = 4 * SLOTS

    def covariances(at):
        buffer = at // step % 2
        values = state_ref[:, at : at + step]
        mean = jnp.sum(values.astype(F32), 0, keepdims=True) / MEMBERS
        for n, (offset, _) in enumerate(tiles):
            covariance = dot(turned_ref[n * SLOTS : (n + 1) * SLOTS], values, ((1,), (0,)))
            for c in range(CAPB):
                row = n * SLOTS + c * OB
                column = (offset + 2) * CAPB + c
                flags = flags_ref[batch_id, column : column + 1, at : at + step]
                total = total_ref[row : row + OB]
                total = jnp.concatenate([total, total], 1)
                kept = (covariance[c * OB : (c + 1) * OB] - total * mean) * flags
                high = kept.astype(BF16)
                low = kept - high.astype(F32)
                kept_ref[buffer, row : row + OB] = high
                low_row = row + (SLOTS if n == 4 else 6 * SLOTS)
                kept_ref[buffer, low_row : low_row + OB] = low.astype(BF16)

    def apply(at):
        buffer = at // step % 2
        change = (
            dot(packs_ref[:, :last], kept_ref[buffer, :last], ((1,), (0,)))
            + dot(packs_ref[:, last:], kept_ref[buffer, last : 6 * SLOTS], ((1,), (0,)))
            + dot(packs_ref[:, :last], kept_ref[buffer, 6 * SLOTS :], ((1,), (0,)))
        )
        values = state_ref[:, at : at + step].astype(F32)
        out_ref[:, at : at + step] = (values + applied(change)).astype(BF16)

    covariances(0)
    for at in range(0, cells, step):
        if at + step < cells:
            covariances(at + step)
        apply(at)


PARAMS = pltpu.CompilerParams(vmem_limit_bytes=32 * 1024 * 1024)
VM = pl.BlockSpec(memory_space=pltpu.VMEM)
SM = pl.BlockSpec(memory_space=pltpu.SMEM)


def observe(block_index, gate_operator, prior_state, groups):
    mem_dev = prior_state.shape[0]
    anywhere = pl.BlockSpec(memory_space=pltpu.HBM)
    return pl.pallas_call(
        observe_kernel,
        in_specs=[anywhere, anywhere, anywhere],
        out_specs=VM,
        out_shape=jax.ShapeDtypeStruct((groups, mem_dev, BATCHES * SLOTS), F32),
        scratch_shapes=[
            pltpu.SMEM(block_index.shape, jnp.int32),
            pltpu.VMEM(gate_operator.shape, F32),
            pltpu.VMEM(prior_state.shape, BF16),
            pltpu.SemaphoreType.DMA(()),
            pltpu.SemaphoreType.DMA(()),
            pltpu.SemaphoreType.DMA(()),
        ],
        compiler_params=pltpu.CompilerParams(vmem_limit_bytes=64 * 1024 * 1024 - 65536),
        name="observe",
    )(block_index, gate_operator, prior_state)


def gather_small(counts, index, local_mask, observed, errors, cells):
    columns = local_mask.shape[2]
    return pl.pallas_call(
        gather_small_kernel,
        in_specs=[SM, SM, VM, VM, VM],
        out_specs=[VM, VM, VM],
        out_shape=[
            jax.ShapeDtypeStruct((columns, SLOTS), F32),
            jax.ShapeDtypeStruct((BATCHES, columns, cells), F32),
            jax.ShapeDtypeStruct((3 * BATCHES, SLOTS), F32),
        ],
        compiler_params=PARAMS,
        name="gather_small",
    )(counts, index, local_mask.transpose(2, 0, 1), observed, errors)


def first_pack(shared, slots):
    return pl.pallas_call(
        first_pack_kernel,
        in_specs=[VM, VM],
        out_specs=VM,
        out_shape=jax.ShapeDtypeStruct((PACK, SLOTS), BF16),
        compiler_params=PARAMS,
        name="first_pack",
    )(shared, slots)


def second_pack(flags, shared, own, around, slots):
    return pl.pallas_call(
        second_pack_kernel,
        in_specs=[VM, VM, VM, VM, VM],
        out_specs=VM,
        out_shape=jax.ShapeDtypeStruct((PACK, SLOTS), BF16),
        compiler_params=PARAMS,
        name="second_pack",
    )(flags, shared, own, around, slots)


def update(batch_id, flags, own, around, state):
    return pl.pallas_call(
        lambda *refs: update_kernel(batch_id, *refs),
        in_specs=[VM, VM, VM, VM],
        out_specs=VM,
        out_shape=jax.ShapeDtypeStruct(state.shape, BF16),
        scratch_shapes=[
            pltpu.VMEM((5 * SLOTS, MEMBERS), BF16),
            pltpu.VMEM((PACK, 6 * SLOTS), BF16),
            pltpu.VMEM((5 * SLOTS, BLK), F32),
            pltpu.VMEM((2, 10 * SLOTS, 2 * BLK), BF16),
        ],
        compiler_params=PARAMS,
        name="update",
    )(flags, own, around, state)


def partner_of(tile, m, across):
    offset = 1 if m % 2 == across else 2
    return tile + offset if tile // offset % 2 == across else tile - offset


def swapped(pack, across, wanted):
    tiles, groups = lax.axis_size("space"), lax.axis_size("mem")
    pairs = []
    for tile in range(tiles):
        for m in range(groups):
            partner = partner_of(tile, m, across)
            if 0 <= partner < tiles and wanted(tile):
                pairs.append((tile * groups + m, partner * groups + m))
    return lax.ppermute(pack, ("space", "mem"), pairs)


def passed_around(pack):
    starts = swapped(pack, 0, lambda tile: tile % ROW < ROW // 2)
    across = swapped(pack, 1, lambda tile: True)
    ends = swapped(pack, 0, lambda tile: tile % ROW >= ROW // 2)
    first = lax.optimization_barrier(jnp.stack([across, starts]))
    return jnp.stack([first[1] + ends, first[0]])


def chip_shared(received):
    groups = lax.axis_size("mem")
    chips = [[2 * chip, 2 * chip + 1] for chip in range(groups // 2)]
    return lax.all_gather(received, "mem", axis=0, axis_index_groups=chips, tiled=True)


def per_device(prior_state, block_counts, block_index, gate_operator, observed, obs_error, local_mask):
    groups = lax.axis_size("mem")
    mem_dev, cells = prior_state.shape
    own_block = observe(block_index, gate_operator, prior_state, groups)
    shared = lax.all_to_all(own_block, "mem", split_axis=0, concat_axis=0, tiled=True)
    prior_state, local_mask, own_block = lax.optimization_barrier((prior_state, local_mask, own_block))
    moved = prior_state.reshape(mem_dev, groups, cells // groups).transpose(1, 0, 2)
    between, flags, slots = gather_small(
        block_counts, block_index, local_mask, observed, obs_error, cells // groups
    )
    moved, between, flags, slots = lax.optimization_barrier((moved, between, flags, slots))
    state = lax.all_to_all(moved, "mem", split_axis=0, concat_axis=0, tiled=True)
    state = state.reshape(MEMBERS, cells // groups)
    pack = first_pack(shared, slots)
    around = chip_shared(passed_around(pack))
    next_pack = second_pack(between, shared, pack, around, slots)
    next_pack, state = lax.optimization_barrier((next_pack, state))
    received = passed_around(next_pack)
    state = update(0, flags, pack, around, state)
    received, state = lax.optimization_barrier((received, state))
    next_around = chip_shared(received)
    state = update(1, flags, next_pack, next_around, state)
    parts = lax.all_to_all(
        state.reshape(groups, mem_dev, cells // groups), "mem", split_axis=0, concat_axis=0, tiled=True
    )
    return parts.transpose(1, 0, 2).reshape(mem_dev, cells)


def solution(mesh):
    placed = (
        P("mem", "space"),
        P(None, "space"),
        P(None, "space"),
        P(None, "space", None, None),
        P(None, "space"),
        P(None, "space"),
        P(None, "space", None),
    )
    return jax.shard_map(
        per_device, mesh=mesh, in_specs=placed, out_specs=P("mem", "space"), check_vma=False
    )
```

```python
import jax
import jax.numpy as jnp
from jax import lax
from jax.experimental import pallas as pl
from jax.experimental.pallas import tpu as pltpu
from jax.sharding import PartitionSpec as P

MEMBERS = 256
ROW = 16
BLK = 128
OB = 32
CAPB = 4
SLOTS = 128
BATCHES = 2
ROWS = 48
PACK = 272
F32 = jnp.float32
BF16 = jnp.bfloat16


def two_parts(value):
    high = value.astype(BF16).astype(F32)
    return high, value - high


def dot(a, b, dims):
    return lax.dot_general(a, b, (dims, ((), ())), preferred_element_type=F32)


def observe_kernel(index_hbm, gate_hbm, state_hbm, out_ref, index_ref, gate, state, index_sem, gate_sem, state_sem):
    index_copy = pltpu.make_async_copy(index_hbm, index_ref, index_sem)
    gate_copy = pltpu.make_async_copy(gate_hbm, gate, gate_sem)
    state_copy = pltpu.make_async_copy(state_hbm, state, state_sem)
    copies = [index_copy, state_copy, gate_copy]
    for copy in copies:
        copy.start()
    for copy in copies:
        copy.wait()
    mem_dev = state.shape[0]
    high, low = two_parts(gate[...].reshape(BATCHES * CAPB * OB, BLK))
    picks = []
    for k in range(BATCHES):
        for c in range(CAPB):
            start = pl.multiple_of(index_ref[k, c] * BLK, BLK)
            picks.append(state[:, pl.ds(start, BLK)])
    rows = jnp.concatenate(picks, 0)
    each = dot(rows, high.astype(BF16), ((1,), (1,))) + dot(rows, low.astype(BF16), ((1,), (1,)))
    lane_block = lax.broadcasted_iota(jnp.int32, (mem_dev, BATCHES * SLOTS), 1) // OB
    prior = jnp.zeros((mem_dev, BATCHES * SLOTS), F32)
    for n in range(BATCHES * CAPB):
        prior = jnp.where(lane_block == n, each[n * mem_dev : (n + 1) * mem_dev], prior)
    mean = jnp.sum(prior, 0, keepdims=True) / mem_dev
    mean_high, mean_low = two_parts(mean)
    row = lax.broadcasted_iota(jnp.int32, (ROWS - mem_dev, BATCHES * SLOTS), 0)
    tail = jnp.where(row == 0, mean_high, jnp.where(row == 1, mean_low, 0.0))
    block = jnp.concatenate([prior - mean, tail], 0).astype(BF16)
    for g in range(out_ref.shape[0]):
        out_ref[g] = block


def gather_small_kernel(counts_ref, index_ref, mask_ref, observed_ref, error_ref, between_ref, own_ref, slots_ref):
    columns, _, blocks = mask_ref.shape
    lane_block = lax.broadcasted_iota(jnp.int32, (1, SLOTS), 1) // OB
    wanted = jnp.zeros((1, SLOTS), jnp.int32)
    for b in range(CAPB):
        wanted = jnp.where(lane_block == b, index_ref[1, b], wanted)
    chosen = (lax.broadcasted_iota(jnp.int32, (blocks, SLOTS), 0) == wanted).astype(F32).astype(BF16)
    mask = mask_ref[...].astype(F32).astype(BF16)
    between_ref[...] = dot(mask[:, 0], chosen, ((1,), (0,)))
    cells = own_ref.shape[2]
    block = lax.broadcasted_iota(jnp.int32, (blocks, cells), 1) // BLK + lax.axis_index("mem") * (cells // BLK)
    mine = (lax.broadcasted_iota(jnp.int32, (blocks, cells), 0) == block).astype(F32).astype(BF16)
    for k in range(BATCHES):
        own_ref[k] = dot(mask[:, k], mine, ((1,), (0,)))
        slots_ref[3 * k : 3 * k + 1] = observed_ref[k : k + 1]
        slots_ref[3 * k + 1 : 3 * k + 2] = error_ref[k : k + 1]
        slots_ref[3 * k + 2 : 3 * k + 3] = (lane_block < counts_ref[k, 0]).astype(F32)


def members_of(shared_ref, batch_id):
    groups = shared_ref.shape[0]
    mem_dev = MEMBERS // groups
    lanes = slice(batch_id * SLOTS, (batch_id + 1) * SLOTS)
    parts = []
    for g in range(groups):
        block = shared_ref[g, :, lanes].astype(F32)
        parts.append(block[:mem_dev] + (block[mem_dev : mem_dev + 1] + block[mem_dev + 1 : mem_dev + 2]))
    return jnp.concatenate(parts, 0)


def store_packed(out_ref, prior, slots):
    observed, error_now, live = slots[0:1], slots[1:2], slots[2:3] > 0.5
    mean_obs = jnp.sum(prior, 0, keepdims=True) / MEMBERS
    spread = prior - mean_obs
    variance = jnp.sum(spread * spread, 0, keepdims=True) / (MEMBERS - 1)
    gain = 1.0 / (variance + error_now)
    shrink = gain / (1.0 + jnp.sqrt(error_now * gain))
    scale = jnp.sqrt(shrink / (MEMBERS - 1))
    level = jnp.where(live, gain * (observed - mean_obs) / (scale * (MEMBERS - 1)), 0.0)
    scaled = (spread * jnp.where(live, scale, 0.0)).astype(BF16)
    total = jnp.sum(scaled.astype(F32), 0, keepdims=True)
    level_high, level_low = two_parts(level)
    total_high, total_low = two_parts(total)
    row = lax.broadcasted_iota(jnp.int32, (PACK - MEMBERS, SLOTS), 0)
    tail = jnp.where(
        row == 0,
        level_high,
        jnp.where(row == 1, level_low, jnp.where(row == 2, total_high, jnp.where(row == 3, total_low, 0.0))),
    )
    out_ref[:MEMBERS] = scaled
    out_ref[MEMBERS:] = tail.astype(BF16)


def first_pack_kernel(shared_ref, slots_ref, out_ref):
    store_packed(out_ref, members_of(shared_ref, 0), slots_ref[0:3])


def window(own_ref, around_ref):
    tile = lax.axis_index("space")
    odd, upper = tile % 2, tile // 2 % 2
    return [
        (0, own_ref),
        (-1, around_ref.at[3 - 3 * odd]),
        (-2, around_ref.at[1 + upper]),
        (1, around_ref.at[3 * odd]),
        (2, around_ref.at[2 - upper]),
    ]


def turned(pack):
    return jnp.transpose(pack[:MEMBERS])


def applied(change):
    return (change[MEMBERS : MEMBERS + 1] + change[MEMBERS + 1 : MEMBERS + 2]) - change[:MEMBERS]


def second_pack_kernel(flags_ref, shared_ref, own_ref, around_ref, slots_ref, out_ref):
    prior = members_of(shared_ref, 1)
    high, low = two_parts(prior - jnp.sum(prior, 0, keepdims=True) / MEMBERS)
    deviation = jnp.concatenate([high, low], 1).astype(BF16)
    tiles = [(offset, pack_ref[...]) for offset, pack_ref in window(own_ref, around_ref)]
    covariance = dot(jnp.concatenate([turned(pack) for _, pack in tiles], 0), deviation, ((1,), (0,)))
    covariance = covariance[:, :SLOTS] + covariance[:, SLOTS:]
    kept = []
    for n, (offset, _) in enumerate(tiles):
        for c in range(CAPB):
            column = (offset + 2) * CAPB + c
            row = n * SLOTS + c * OB
            kept.append(covariance[row : row + OB] * flags_ref[column : column + 1])
    high, low = two_parts(jnp.concatenate(kept, 0))
    parts = jnp.concatenate([high, low], 1).astype(BF16)
    change = dot(jnp.concatenate([pack for _, pack in tiles], 1), parts, ((1,), (0,)))
    prior = prior + applied(change[:, :SLOTS] + change[:, SLOTS:])
    store_packed(out_ref, prior, slots_ref[3:6])


def update_kernel(
    batch_id, flags_ref, own_ref, around_ref, state_ref, out_ref, turned_ref, packs_ref, total_ref, kept_ref
):
    tiles = window(own_ref, around_ref)
    for n, (_, pack_ref) in enumerate(tiles):
        span = slice(n * SLOTS, (n + 1) * SLOTS)
        turned_ref[span] = turned(pack_ref[...])
        packs_ref[:, span] = pack_ref[...]
    packs_ref[:, 5 * SLOTS :] = tiles[4][1][...]
    total_ref[...] = dot(turned_ref[...], jnp.ones((MEMBERS, BLK), BF16), ((1,), (0,)))
    cells = state_ref.shape[1]
    step = 2 * BLK
    last = 4 * SLOTS

    def covariances(at):
        buffer = at // step % 2
        values = state_ref[:, at : at + step]
        mean = jnp.sum(values.astype(F32), 0, keepdims=True) / MEMBERS
        for n, (offset, _) in enumerate(tiles):
            covariance = dot(turned_ref[n * SLOTS : (n + 1) * SLOTS], values, ((1,), (0,)))
            for c in range(CAPB):
                row = n * SLOTS + c * OB
                column = (offset + 2) * CAPB + c
                flags = flags_ref[batch_id, column : column + 1, at : at + step]
                total = total_ref[row : row + OB]
                total = jnp.concatenate([total, total], 1)
                kept = (covariance[c * OB : (c + 1) * OB] - total * mean) * flags
                high = kept.astype(BF16)
                low = kept - high.astype(F32)
                kept_ref[buffer, row : row + OB] = high
                low_row = row + (SLOTS if n == 4 else 6 * SLOTS)
                kept_ref[buffer, low_row : low_row + OB] = low.astype(BF16)

    def apply(at):
        buffer = at // step % 2
        change = (
            dot(packs_ref[:, :last], kept_ref[buffer, :last], ((1,), (0,)))
            + dot(packs_ref[:, last:], kept_ref[buffer, last : 6 * SLOTS], ((1,), (0,)))
            + dot(packs_ref[:, :last], kept_ref[buffer, 6 * SLOTS :], ((1,), (0,)))
        )
        values = state_ref[:, at : at + step].astype(F32)
        out_ref[:, at : at + step] = (values + applied(change)).astype(BF16)

    covariances(0)
    for at in range(0, cells, step):
        if at + step < cells:
            covariances(at + step)
        apply(at)


PARAMS = pltpu.CompilerParams(vmem_limit_bytes=32 * 1024 * 1024)
VM = pl.BlockSpec(memory_space=pltpu.VMEM)
SM = pl.BlockSpec(memory_space=pltpu.SMEM)


def observe(block_index, gate_operator, prior_state, groups):
    mem_dev = prior_state.shape[0]
    anywhere = pl.BlockSpec(memory_space=pltpu.HBM)
    return pl.pallas_call(
        observe_kernel,
        in_specs=[anywhere, anywhere, anywhere],
        out_specs=VM,
        out_shape=jax.ShapeDtypeStruct((groups, ROWS, BATCHES * SLOTS), BF16),
        scratch_shapes=[
            pltpu.SMEM(block_index.shape, jnp.int32),
            pltpu.VMEM(gate_operator.shape, F32),
            pltpu.VMEM(prior_state.shape, BF16),
            pltpu.SemaphoreType.DMA(()),
            pltpu.SemaphoreType.DMA(()),
            pltpu.SemaphoreType.DMA(()),
        ],
        compiler_params=pltpu.CompilerParams(vmem_limit_bytes=64 * 1024 * 1024 - 65536),
        name="observe",
    )(block_index, gate_operator, prior_state)


def gather_small(counts, index, local_mask, observed, errors, cells):
    columns = local_mask.shape[2]
    return pl.pallas_call(
        gather_small_kernel,
        in_specs=[SM, SM, VM, VM, VM],
        out_specs=[VM, VM, VM],
        out_shape=[
            jax.ShapeDtypeStruct((columns, SLOTS), F32),
            jax.ShapeDtypeStruct((BATCHES, columns, cells), F32),
            jax.ShapeDtypeStruct((3 * BATCHES, SLOTS), F32),
        ],
        compiler_params=PARAMS,
        name="gather_small",
    )(counts, index, local_mask.transpose(2, 0, 1), observed, errors)


def first_pack(shared, slots):
    return pl.pallas_call(
        first_pack_kernel,
        in_specs=[VM, VM],
        out_specs=VM,
        out_shape=jax.ShapeDtypeStruct((PACK, SLOTS), BF16),
        compiler_params=PARAMS,
        name="first_pack",
    )(shared, slots)


def second_pack(flags, shared, own, around, slots):
    return pl.pallas_call(
        second_pack_kernel,
        in_specs=[VM, VM, VM, VM, VM],
        out_specs=VM,
        out_shape=jax.ShapeDtypeStruct((PACK, SLOTS), BF16),
        compiler_params=PARAMS,
        name="second_pack",
    )(flags, shared, own, around, slots)


def update(batch_id, flags, own, around, state):
    return pl.pallas_call(
        lambda *refs: update_kernel(batch_id, *refs),
        in_specs=[VM, VM, VM, VM],
        out_specs=VM,
        out_shape=jax.ShapeDtypeStruct(state.shape, BF16),
        scratch_shapes=[
            pltpu.VMEM((5 * SLOTS, MEMBERS), BF16),
            pltpu.VMEM((PACK, 6 * SLOTS), BF16),
            pltpu.VMEM((5 * SLOTS, BLK), F32),
            pltpu.VMEM((2, 10 * SLOTS, 2 * BLK), BF16),
        ],
        compiler_params=PARAMS,
        name="update",
    )(flags, own, around, state)


def partner_of(tile, m, across):
    offset = 1 if m % 2 == across else 2
    return tile + offset if tile // offset % 2 == across else tile - offset


def swapped(pack, across, wanted):
    tiles, groups = lax.axis_size("space"), lax.axis_size("mem")
    pairs = []
    for tile in range(tiles):
        for m in range(groups):
            partner = partner_of(tile, m, across)
            if 0 <= partner < tiles and wanted(tile):
                pairs.append((tile * groups + m, partner * groups + m))
    return lax.ppermute(pack, ("space", "mem"), pairs)


def passed_around(pack):
    starts = swapped(pack, 0, lambda tile: tile % ROW < ROW // 2)
    across = swapped(pack, 1, lambda tile: True)
    ends = swapped(pack, 0, lambda tile: tile % ROW >= ROW // 2)
    first = lax.optimization_barrier(jnp.stack([across, starts]))
    return jnp.stack([first[1] + ends, first[0]])


def chip_shared(received):
    groups = lax.axis_size("mem")
    chips = [[2 * chip, 2 * chip + 1] for chip in range(groups // 2)]
    return lax.all_gather(received, "mem", axis=0, axis_index_groups=chips, tiled=True)


def per_device(prior_state, block_counts, block_index, gate_operator, observed, obs_error, local_mask):
    groups = lax.axis_size("mem")
    mem_dev, cells = prior_state.shape
    own_block = observe(block_index, gate_operator, prior_state, groups)
    shared = lax.all_to_all(own_block, "mem", split_axis=0, concat_axis=0, tiled=True)
    prior_state, local_mask, own_block = lax.optimization_barrier((prior_state, local_mask, own_block))
    moved = prior_state.reshape(mem_dev, groups, cells // groups).transpose(1, 0, 2)
    between, flags, slots = gather_small(
        block_counts, block_index, local_mask, observed, obs_error, cells // groups
    )
    moved, between, flags, slots = lax.optimization_barrier((moved, between, flags, slots))
    state = lax.all_to_all(moved, "mem", split_axis=0, concat_axis=0, tiled=True)
    state = state.reshape(MEMBERS, cells // groups)
    pack = first_pack(shared, slots)
    around = chip_shared(passed_around(pack))
    next_pack = second_pack(between, shared, pack, around, slots)
    next_pack, state = lax.optimization_barrier((next_pack, state))
    received = passed_around(next_pack)
    state = update(0, flags, pack, around, state)
    received, state = lax.optimization_barrier((received, state))
    next_around = chip_shared(received)
    state = update(1, flags, next_pack, next_around, state)
    parts = lax.all_to_all(
        state.reshape(groups, mem_dev, cells // groups), "mem", split_axis=0, concat_axis=0, tiled=True
    )
    return parts.transpose(1, 0, 2).reshape(mem_dev, cells)


def solution(mesh):
    placed = (
        P("mem", "space"),
        P(None, "space"),
        P(None, "space"),
        P(None, "space", None, None),
        P(None, "space"),
        P(None, "space"),
        P(None, "space", None),
    )
    return jax.shard_map(
        per_device, mesh=mesh, in_specs=placed, out_specs=P("mem", "space"), check_vma=False
    )
```

```python
import jax
import jax.numpy as jnp
from jax import lax
from jax.experimental import pallas as pl
from jax.experimental.pallas import tpu as pltpu
from jax.sharding import PartitionSpec as P

MEMBERS = 256
ROW = 16
BLK = 128
OB = 32
CAPB = 4
SLOTS = 128
BATCHES = 2
ROWS = 48
PACK = 272
F32 = jnp.float32
BF16 = jnp.bfloat16


def two_parts(value):
    high = value.astype(BF16).astype(F32)
    return high, value - high


def dot(a, b, dims):
    return lax.dot_general(a, b, (dims, ((), ())), preferred_element_type=F32)


def observe_kernel(index_hbm, gate_hbm, state_hbm, out_ref, index_ref, gate, state, index_sem, gate_sem, state_sem):
    index_copy = pltpu.make_async_copy(index_hbm, index_ref, index_sem)
    gate_copy = pltpu.make_async_copy(gate_hbm, gate, gate_sem)
    state_copy = pltpu.make_async_copy(state_hbm, state, state_sem)
    copies = [index_copy, state_copy, gate_copy]
    for copy in copies:
        copy.start()
    for copy in copies:
        copy.wait()
    mem_dev = state.shape[0]
    high, low = two_parts(gate[...].reshape(BATCHES * CAPB * OB, BLK))
    picks = []
    for k in range(BATCHES):
        for c in range(CAPB):
            start = pl.multiple_of(index_ref[k, c] * BLK, BLK)
            picks.append(state[:, pl.ds(start, BLK)])
    rows = jnp.concatenate(picks, 0)
    each = dot(rows, high.astype(BF16), ((1,), (1,))) + dot(rows, low.astype(BF16), ((1,), (1,)))
    lane_block = lax.broadcasted_iota(jnp.int32, (mem_dev, BATCHES * SLOTS), 1) // OB
    prior = jnp.zeros((mem_dev, BATCHES * SLOTS), F32)
    for n in range(BATCHES * CAPB):
        prior = jnp.where(lane_block == n, each[n * mem_dev : (n + 1) * mem_dev], prior)
    mean = jnp.sum(prior, 0, keepdims=True) / mem_dev
    mean_high, mean_low = two_parts(mean)
    row = lax.broadcasted_iota(jnp.int32, (ROWS - mem_dev, BATCHES * SLOTS), 0)
    tail = jnp.where(row == 0, mean_high, jnp.where(row == 1, mean_low, 0.0))
    block = jnp.concatenate([prior - mean, tail], 0).astype(BF16)
    for g in range(out_ref.shape[0]):
        out_ref[g] = block


def gather_small_kernel(counts_ref, index_ref, mask_ref, observed_ref, error_ref, between_ref, own_ref, slots_ref):
    columns, _, blocks = mask_ref.shape
    lane_block = lax.broadcasted_iota(jnp.int32, (1, SLOTS), 1) // OB
    wanted = jnp.zeros((1, SLOTS), jnp.int32)
    for b in range(CAPB):
        wanted = jnp.where(lane_block == b, index_ref[1, b], wanted)
    chosen = (lax.broadcasted_iota(jnp.int32, (blocks, SLOTS), 0) == wanted).astype(F32).astype(BF16)
    mask = mask_ref[...].astype(F32).astype(BF16)
    between_ref[...] = dot(mask[:, 0], chosen, ((1,), (0,)))
    cells = own_ref.shape[2]
    block = lax.broadcasted_iota(jnp.int32, (blocks, cells), 1) // BLK + lax.axis_index("mem") * (cells // BLK)
    mine = (lax.broadcasted_iota(jnp.int32, (blocks, cells), 0) == block).astype(F32).astype(BF16)
    for k in range(BATCHES):
        own_ref[k] = dot(mask[:, k], mine, ((1,), (0,)))
        slots_ref[3 * k : 3 * k + 1] = observed_ref[k : k + 1]
        slots_ref[3 * k + 1 : 3 * k + 2] = error_ref[k : k + 1]
        slots_ref[3 * k + 2 : 3 * k + 3] = (lane_block < counts_ref[k, 0]).astype(F32)


def members_of(shared_ref, batch_id):
    groups = shared_ref.shape[0]
    mem_dev = MEMBERS // groups
    lanes = slice(batch_id * SLOTS, (batch_id + 1) * SLOTS)
    parts = []
    for g in range(groups):
        block = shared_ref[g, :, lanes].astype(F32)
        parts.append(block[:mem_dev] + (block[mem_dev : mem_dev + 1] + block[mem_dev + 1 : mem_dev + 2]))
    return jnp.concatenate(parts, 0)


def store_packed(out_ref, prior, slots):
    observed, error_now, live = slots[0:1], slots[1:2], slots[2:3] > 0.5
    mean_obs = jnp.sum(prior, 0, keepdims=True) / MEMBERS
    spread = prior - mean_obs
    variance = jnp.sum(spread * spread, 0, keepdims=True) / (MEMBERS - 1)
    gain = 1.0 / (variance + error_now)
    shrink = gain / (1.0 + jnp.sqrt(error_now * gain))
    scale = jnp.sqrt(shrink / (MEMBERS - 1))
    level = jnp.where(live, gain * (observed - mean_obs) / (scale * (MEMBERS - 1)), 0.0)
    scaled = (spread * jnp.where(live, scale, 0.0)).astype(BF16)
    total = jnp.sum(scaled.astype(F32), 0, keepdims=True)
    level_high, level_low = two_parts(level)
    total_high, total_low = two_parts(total)
    row = lax.broadcasted_iota(jnp.int32, (PACK - MEMBERS, SLOTS), 0)
    tail = jnp.where(
        row == 0,
        level_high,
        jnp.where(row == 1, level_low, jnp.where(row == 2, total_high, jnp.where(row == 3, total_low, 0.0))),
    )
    out_ref[:MEMBERS] = scaled
    out_ref[MEMBERS:] = tail.astype(BF16)


def first_pack_kernel(shared_ref, slots_ref, out_ref):
    store_packed(out_ref, members_of(shared_ref, 0), slots_ref[0:3])


def window(own_ref, around_ref):
    tile = lax.axis_index("space")
    odd, upper = tile % 2, tile // 2 % 2
    return [
        (0, own_ref),
        (-1, around_ref.at[3 - 3 * odd]),
        (-2, around_ref.at[1 + upper]),
        (1, around_ref.at[3 * odd]),
        (2, around_ref.at[2 - upper]),
    ]


def turned(pack):
    return jnp.transpose(pack[:MEMBERS])


def applied(change):
    return (change[MEMBERS : MEMBERS + 1] + change[MEMBERS + 1 : MEMBERS + 2]) - change[:MEMBERS]


def second_pack_kernel(flags_ref, shared_ref, own_ref, around_ref, slots_ref, out_ref):
    prior = members_of(shared_ref, 1)
    high, low = two_parts(prior - jnp.sum(prior, 0, keepdims=True) / MEMBERS)
    deviation = jnp.concatenate([high, low], 1).astype(BF16)
    tiles = [(offset, pack_ref[...]) for offset, pack_ref in window(own_ref, around_ref)]
    covariance = dot(jnp.concatenate([turned(pack) for _, pack in tiles], 0), deviation, ((1,), (0,)))
    covariance = covariance[:, :SLOTS] + covariance[:, SLOTS:]
    kept = []
    for n, (offset, _) in enumerate(tiles):
        for c in range(CAPB):
            column = (offset + 2) * CAPB + c
            row = n * SLOTS + c * OB
            kept.append(covariance[row : row + OB] * flags_ref[column : column + 1])
    high, low = two_parts(jnp.concatenate(kept, 0))
    parts = jnp.concatenate([high, low], 1).astype(BF16)
    change = dot(jnp.concatenate([pack for _, pack in tiles], 1), parts, ((1,), (0,)))
    prior = prior + applied(change[:, :SLOTS] + change[:, SLOTS:])
    store_packed(out_ref, prior, slots_ref[3:6])


def update_kernel(
    batch_id, flags_ref, own_ref, around_ref, state_ref, mean_ref, out_ref, turned_ref, packs_ref, total_ref, kept_ref
):
    tiles = window(own_ref, around_ref)
    for n, (_, pack_ref) in enumerate(tiles):
        span = slice(n * SLOTS, (n + 1) * SLOTS)
        turned_ref[span] = turned(pack_ref[...])
        packs_ref[:, span] = pack_ref[...]
    packs_ref[:, 5 * SLOTS :] = tiles[4][1][...]
    total_ref[...] = dot(turned_ref[...], jnp.ones((MEMBERS, BLK), BF16), ((1,), (0,)))
    cells = state_ref.shape[1]
    step = 2 * BLK
    last = 4 * SLOTS

    def covariances(at):
        buffer = at // step % 2
        values = state_ref[:, at : at + step]
        if batch_id == 0:
            mean = jnp.sum(values.astype(F32), 0, keepdims=True) / MEMBERS
        else:
            mean = mean_ref[0:1, at : at + step]
        for n, (offset, _) in enumerate(tiles):
            covariance = dot(turned_ref[n * SLOTS : (n + 1) * SLOTS], values, ((1,), (0,)))
            for c in range(CAPB):
                row = n * SLOTS + c * OB
                column = (offset + 2) * CAPB + c
                flags = flags_ref[batch_id, column : column + 1, at : at + step]
                total = total_ref[row : row + OB]
                total = jnp.concatenate([total, total], 1)
                kept = (covariance[c * OB : (c + 1) * OB] - total * mean) * flags
                high = kept.astype(BF16)
                low = kept - high.astype(F32)
                kept_ref[buffer, row : row + OB] = high
                low_row = row + (SLOTS if n == 4 else 6 * SLOTS)
                kept_ref[buffer, low_row : low_row + OB] = low.astype(BF16)

    def apply(at):
        buffer = at // step % 2
        change = (
            dot(packs_ref[:, :last], kept_ref[buffer, :last], ((1,), (0,)))
            + dot(packs_ref[:, last:], kept_ref[buffer, last : 6 * SLOTS], ((1,), (0,)))
            + dot(packs_ref[:, :last], kept_ref[buffer, 6 * SLOTS :], ((1,), (0,)))
        )
        values = state_ref[:, at : at + step].astype(F32)
        values = (values + applied(change)).astype(BF16)
        out_ref[:, at : at + step] = values
        if batch_id == 0:
            mean_ref[:, at : at + step] = jnp.sum(values.astype(F32), 0, keepdims=True) / MEMBERS

    covariances(0)
    for at in range(0, cells, step):
        if at + step < cells:
            covariances(at + step)
        apply(at)


PARAMS = pltpu.CompilerParams(vmem_limit_bytes=32 * 1024 * 1024)
VM = pl.BlockSpec(memory_space=pltpu.VMEM)
SM = pl.BlockSpec(memory_space=pltpu.SMEM)


def observe(block_index, gate_operator, prior_state, groups):
    mem_dev = prior_state.shape[0]
    anywhere = pl.BlockSpec(memory_space=pltpu.HBM)
    return pl.pallas_call(
        observe_kernel,
        in_specs=[anywhere, anywhere, anywhere],
        out_specs=VM,
        out_shape=jax.ShapeDtypeStruct((groups, ROWS, BATCHES * SLOTS), BF16),
        scratch_shapes=[
            pltpu.SMEM(block_index.shape, jnp.int32),
            pltpu.VMEM(gate_operator.shape, F32),
            pltpu.VMEM(prior_state.shape, BF16),
            pltpu.SemaphoreType.DMA(()),
            pltpu.SemaphoreType.DMA(()),
            pltpu.SemaphoreType.DMA(()),
        ],
        compiler_params=pltpu.CompilerParams(vmem_limit_bytes=64 * 1024 * 1024 - 65536),
        name="observe",
    )(block_index, gate_operator, prior_state)


def gather_small(counts, index, local_mask, observed, errors, cells):
    columns = local_mask.shape[2]
    return pl.pallas_call(
        gather_small_kernel,
        in_specs=[SM, SM, VM, VM, VM],
        out_specs=[VM, VM, VM],
        out_shape=[
            jax.ShapeDtypeStruct((columns, SLOTS), F32),
            jax.ShapeDtypeStruct((BATCHES, columns, cells), F32),
            jax.ShapeDtypeStruct((3 * BATCHES, SLOTS), F32),
        ],
        compiler_params=PARAMS,
        name="gather_small",
    )(counts, index, local_mask.transpose(2, 0, 1), observed, errors)


def first_pack(shared, slots):
    return pl.pallas_call(
        first_pack_kernel,
        in_specs=[VM, VM],
        out_specs=VM,
        out_shape=jax.ShapeDtypeStruct((PACK, SLOTS), BF16),
        compiler_params=PARAMS,
        name="first_pack",
    )(shared, slots)


def second_pack(flags, shared, own, around, slots):
    return pl.pallas_call(
        second_pack_kernel,
        in_specs=[VM, VM, VM, VM, VM],
        out_specs=VM,
        out_shape=jax.ShapeDtypeStruct((PACK, SLOTS), BF16),
        compiler_params=PARAMS,
        name="second_pack",
    )(flags, shared, own, around, slots)


def first_update_kernel(flags_ref, own_ref, around_ref, state_ref, out_ref, mean_ref, *scratch):
    update_kernel(0, flags_ref, own_ref, around_ref, state_ref, mean_ref, out_ref, *scratch)


def second_update_kernel(flags_ref, own_ref, around_ref, state_ref, mean_ref, out_ref, *scratch):
    update_kernel(1, flags_ref, own_ref, around_ref, state_ref, mean_ref, out_ref, *scratch)


def update(kernel, flags, own, around, state, *mean):
    shape = jax.ShapeDtypeStruct(state.shape, BF16)
    means = jax.ShapeDtypeStruct((1, state.shape[1]), F32)
    return pl.pallas_call(
        kernel,
        in_specs=[VM] * (4 + len(mean)),
        out_specs=VM if mean else [VM, VM],
        out_shape=shape if mean else [shape, means],
        scratch_shapes=[
            pltpu.VMEM((5 * SLOTS, MEMBERS), BF16),
            pltpu.VMEM((PACK, 6 * SLOTS), BF16),
            pltpu.VMEM((5 * SLOTS, BLK), F32),
            pltpu.VMEM((2, 10 * SLOTS, 2 * BLK), BF16),
        ],
        compiler_params=PARAMS,
        name="update",
    )(flags, own, around, state, *mean)


def partner_of(tile, m, across):
    offset = 1 if m % 2 == across else 2
    return tile + offset if tile // offset % 2 == across else tile - offset


def swapped(pack, across, wanted):
    tiles, groups = lax.axis_size("space"), lax.axis_size("mem")
    pairs = []
    for tile in range(tiles):
        for m in range(groups):
            partner = partner_of(tile, m, across)
            if 0 <= partner < tiles and wanted(tile):
                pairs.append((tile * groups + m, partner * groups + m))
    return lax.ppermute(pack, ("space", "mem"), pairs)


def passed_around(pack):
    starts = swapped(pack, 0, lambda tile: tile % ROW < ROW // 2)
    across = swapped(pack, 1, lambda tile: True)
    ends = swapped(pack, 0, lambda tile: tile % ROW >= ROW // 2)
    first = lax.optimization_barrier(jnp.stack([across, starts]))
    return jnp.stack([first[1] + ends, first[0]])


def chip_shared(received):
    groups = lax.axis_size("mem")
    chips = [[2 * chip, 2 * chip + 1] for chip in range(groups // 2)]
    return lax.all_gather(received, "mem", axis=0, axis_index_groups=chips, tiled=True)


def per_device(prior_state, block_counts, block_index, gate_operator, observed, obs_error, local_mask):
    groups = lax.axis_size("mem")
    mem_dev, cells = prior_state.shape
    own_block = observe(block_index, gate_operator, prior_state, groups)
    shared = lax.all_to_all(own_block, "mem", split_axis=0, concat_axis=0, tiled=True)
    prior_state, local_mask, own_block = lax.optimization_barrier((prior_state, local_mask, own_block))
    moved = prior_state.reshape(mem_dev, groups, cells // groups).transpose(1, 0, 2)
    between, flags, slots = gather_small(
        block_counts, block_index, local_mask, observed, obs_error, cells // groups
    )
    moved, between, flags, slots = lax.optimization_barrier((moved, between, flags, slots))
    state = lax.all_to_all(moved, "mem", split_axis=0, concat_axis=0, tiled=True)
    state = state.reshape(MEMBERS, cells // groups)
    pack = first_pack(shared, slots)
    around = chip_shared(passed_around(pack))
    next_pack = second_pack(between, shared, pack, around, slots)
    next_pack, state = lax.optimization_barrier((next_pack, state))
    received = passed_around(next_pack)
    state, mean = update(first_update_kernel, flags, pack, around, state)
    received, state, mean = lax.optimization_barrier((received, state, mean))
    next_around = chip_shared(received)
    state = update(second_update_kernel, flags, next_pack, next_around, state, mean)
    parts = lax.all_to_all(
        state.reshape(groups, mem_dev, cells // groups), "mem", split_axis=0, concat_axis=0, tiled=True
    )
    return parts.transpose(1, 0, 2).reshape(mem_dev, cells)


def solution(mesh):
    placed = (
        P("mem", "space"),
        P(None, "space"),
        P(None, "space"),
        P(None, "space", None, None),
        P(None, "space"),
        P(None, "space"),
        P(None, "space", None),
    )
    return jax.shard_map(
        per_device, mesh=mesh, in_specs=placed, out_specs=P("mem", "space"), check_vma=False
    )
```
